256 devices in a mesh: row: 64 (over z, y_hi, x), ka: 4 (over y_lo, core).
Axes of the slice: x: 4, y: 4 (y_hi: 2, y_lo: 2; y = y_hi * 2 + y_lo), z: 8, core: 2. Of those that a mesh axis runs over, the one named last changes fastest.
Arguments:
- pair: bfloat16 [256, 256, 128], P('row', 'ka'), may hold values from -6 to 6
- token_mask: int32 [256], replicated, may hold values 0 or 1
- w_proj: bfloat16 [2, 128, 640], replicated, may hold values from -0.5 to 0.5
- w_out: bfloat16 [2, 128, 128], replicated, may hold values from -0.5 to 0.5
Outputs:
- pair_out: bfloat16 [256, 256, 128], P('row', 'ka')
The draws below stay inside these ranges and needn't reach their ends.
Inputs may be any that keep to these rules, and one draw needn't show every extreme that they name: `token_mask`: 1 marks a real token, 0 a padding token.
All inputs are finite; a program needn't handle non-finite values.
Results may differ from the reference program's by a relative error of at most 0.018.
Values may be sent and summed in bfloat16 or wider, within the bound.
A program may use at most 64 MiB of HBM per device.

```python
import jax
import jax.numpy as jnp
from jax import lax

PAIR_CH = 128
TRI_CH = 128
TOKENS = 256


def place_ends(drawn, stream_key, smallest, largest):
    shape = drawn.shape
    index_at = [jax.random.randint(jax.random.fold_in(stream_key, axis), (), 0, shape[axis]) for axis in range(len(shape))]
    drawn = drawn.at[tuple(index_at)].set(smallest)
    longest = shape.index(max(shape))
    index_at[longest] = (index_at[longest] + 1) % shape[longest]
    return drawn.at[tuple(index_at)].set(largest)


def level_of(rng, extent, split, least, largest):
    def one(position, blocks):
        steps = jax.random.uniform(jax.random.fold_in(jax.random.fold_in(rng, 6), position), (blocks,), jnp.float32, least / len(split), largest / len(split))
        return jnp.repeat(jnp.exp(steps), extent[position] // blocks).reshape((-1,) + (1,) * (len(extent) - position - 1))

    loudness = one(*split[0])
    for cut in split[1:]:
        loudness = loudness * one(*cut)
    return loudness


def normal_values(rng, dims, spread, reach, cuts=(), kind=jnp.bfloat16):
    drawn = spread * jax.random.normal(rng, dims, jnp.float32)
    if cuts:
        drawn = drawn * level_of(rng, dims, cuts, -0.22, 0.18)
    return jnp.clip(drawn, -reach, reach).astype(kind)


def setup_inputs(seed: int = 0) -> dict:
    seeds = jax.random.split(jax.random.key(seed), 5)
    return {
        "pair": normal_values(seeds[0], (TOKENS, TOKENS, PAIR_CH), 1.0, 6.0, ((0, 64), (1, 4))),
        "token_mask": place_ends((jax.random.randint(seeds[1], (TOKENS,), 0, 8) < 7).astype(jnp.int32), jax.random.fold_in(seeds[1], 1), 0, 1),
        "w_proj": normal_values(seeds[2], (2, PAIR_CH, 4 * TRI_CH + PAIR_CH), PAIR_CH ** -0.5, 0.5),
        "w_out": normal_values(seeds[3], (2, TRI_CH, PAIR_CH), TRI_CH ** -0.5, 0.5),
    }


epsilon = 1e-05

def normalize(values):
    mean = lax.optimization_barrier(jnp.mean(values, axis=-1, keepdims=True))
    centered = values - mean
    variance = lax.optimization_barrier(jnp.mean(centered * centered, axis=-1, keepdims=True))
    return centered * lax.rsqrt(variance + epsilon)

def reference(pair, token_mask, w_proj, w_out):
    token_weights = token_mask.astype(jnp.float32)
    pair_mask = token_weights[:, None] * token_weights[None, :]
    hidden = w_out.shape[1]
    channels = pair.shape[2]
    count = pair.shape[0]
    for section_index, pattern in ((0, 'ikc,jkc->ijc'), (1, 'kic,kjc->ijc')):
        normed = normalize(pair.astype(jnp.float32)).astype(jnp.bfloat16)
        projected = jnp.dot(normed.reshape(-1, channels), w_proj[section_index], preferred_element_type=jnp.float32)
        projected = projected.reshape(count, count, -1)
        left_side = (jax.nn.sigmoid(projected[..., :hidden]) * projected[..., hidden:2 * hidden] * pair_mask[..., None]).astype(jnp.bfloat16)
        right_side = (jax.nn.sigmoid(projected[..., 2 * hidden:3 * hidden]) * projected[..., 3 * hidden:4 * hidden] * pair_mask[..., None]).astype(jnp.bfloat16)
        gate_out = jax.nn.sigmoid(projected[..., 4 * hidden:])
        summed = jnp.einsum(pattern, left_side.astype(jnp.float32), right_side.astype(jnp.float32), precision=lax.Precision.HIGHEST)
        xnorm = normalize(summed).astype(jnp.bfloat16)
        update = jnp.dot(xnorm.reshape(-1, hidden), w_out[section_index], preferred_element_type=jnp.float32).reshape(count, count, channels)
        pair = (pair.astype(jnp.float32) + gate_out * update).astype(jnp.bfloat16)
    return pair
```

```python
import functools

import jax
import jax.numpy as jnp
from jax import lax
from jax.experimental import pallas as pl
from jax.experimental.pallas import tpu as pltpu
from jax.sharding import PartitionSpec as P

EPS = 1e-05
MESH = pl.DeviceIdType.MESH
NEAR = (8, 9, 7, 10, 6, 5, 11, 12, 4, 3, 13, 14, 2, 1, 15)
F32 = jnp.float32
BF16 = jnp.bfloat16
NT = (((1,), (1,)), ((), ()))
NN = (((1,), (0,)), ((), ()))


def dot(a, b, dims):
    return lax.dot_general(a, b, dims, preferred_element_type=F32)


def iota(shape, axis):
    return lax.broadcasted_iota(jnp.int32, shape, axis)


def onehot(cond):
    return jnp.where(cond, 1.0, 0.0).astype(BF16)


def column_of(p):
    return (
        32 * ((p // 4) % 2)
        + 16 * ((p // 2) % 2)
        + 4 * (p // 16)
        + 2 * (p % 2)
        + (p // 8) % 2
    )


def eye(n):
    return onehot(iota((n, n), 0) == iota((n, n), 1))


def norm_t(v):
    mean = jnp.mean(v, axis=0, keepdims=True)
    centered = v - mean
    var = jnp.mean(centered * centered, axis=0, keepdims=True)
    return centered * lax.rsqrt(var + EPS)


def transposed_weight(w, lo):
    return dot(eye(128), w[:, lo : lo + 128], NT).astype(BF16)


def tiles_of(t):
    lo = t[:, :128].reshape(16, 8, 128)
    hi = t[:, 128:].reshape(16, 8, 128)
    return jnp.concatenate([lo, hi], axis=1).astype(BF16)


def kernel(
    pair, mask, wp, wo, out,
    xb, mb, wpb, wob, wt, p_t, gate,
    send1, recv1, scratch, la0, ra0, lb0, rb0, la1, ra1, lb1, rb1, osend, orecv,
    lsem, s1s, s1r, l2s, l2r, r2s, r2r, os, orr,
):
    row = lax.axis_index("row")
    q = lax.axis_index("ka")
    g = row // 4
    x = row % 4
    s = x * 4 + q

    barrier = pltpu.get_barrier_semaphore()
    for d in NEAR:
        pl.semaphore_signal(
            barrier, inc=1, device_id=(((g + d) % 16) * 4 + x, q), device_id_type=MESH
        )
        t = (s + d) % 16
        pl.semaphore_signal(
            barrier, inc=1, device_id=(g * 4 + t // 4, t % 4), device_id_type=MESH
        )
    loads = [
        pltpu.make_async_copy(a, b, lsem.at[i])
        for i, (a, b) in enumerate(((pair, xb), (mask, mb), (wp, wpb), (wo, wob)))
    ]
    for c in loads:
        c.start()
    for c in loads:
        c.wait()

    for u in range(2):
        for blk in range(5):
            wt[u, blk] = transposed_weight(wpb[u], blk * 128)
        wt[u, 5] = transposed_weight(wob[u], 0)

    n0 = iota((256, 256), 0)
    n1 = iota((256, 256), 1)
    perm_t = onehot(n1 == (n0 // 64) * 64 + column_of(n0 % 64))
    perm = onehot(n0 == (n1 // 64) * 64 + column_of(n1 % 64))
    moved = dot(perm_t, xb[...].reshape(256, 128), NN).astype(BF16)
    p_t[...] = dot(eye(128), moved, NT)
    tokens = jnp.broadcast_to(mb[...].astype(F32), (16, 256)).astype(BF16)
    m_row = dot(tokens, onehot(n0 == 4 * row + n1 // 64), NN)[0:1]
    m_col = dot(tokens, onehot(n0 == 64 * q + column_of(n1 % 64)), NN)[0:1]
    m_pair = m_row * m_col

    def project(u):
        normed = norm_t(p_t[...]).astype(BF16)
        ga = dot(wt[u, 0], normed, NN)
        va = dot(wt[u, 1], normed, NN)
        send1[u, :, 0] = tiles_of(jax.nn.sigmoid(ga) * va * m_pair)
        gb = dot(wt[u, 2], normed, NN)
        vb = dot(wt[u, 3], normed, NN)
        send1[u, :, 1] = tiles_of(jax.nn.sigmoid(gb) * vb * m_pair)

    def gate_of(u):
        normed = norm_t(p_t[...]).astype(BF16)
        gate[...] = jax.nn.sigmoid(dot(wt[u, 4], normed, NN))

    def exchange1(src, dst, ssem, rsem):
        for d in NEAR:
            t = (g + d) % 16
            pltpu.make_async_remote_copy(
                src.at[t], dst.at[g], ssem, rsem, device_id=(t * 4 + x, q), device_id_type=MESH
            ).start()
        dst[g] = src[g]

    def wait_bytes(buf, count, ssem, rsem, send):
        part = buf.at[pl.ds(0, count)]
        c = pltpu.make_async_remote_copy(
            part, part, ssem, rsem, device_id=(g * 4 + (x + 1) % 4, q), device_id_type=MESH
        )
        if send:
            c.wait_send()
        else:
            c.wait_recv()

    low = iota((32, 128), 1) < 64

    def pairs(u, side, cp):
        f = scratch.at[side]
        xa = f[pl.ds(2 * cp, 32, stride=8), :]
        xb_ = f[pl.ds(2 * cp + 1, 32, stride=8), :]
        even = jnp.where(low, xa, pltpu.roll(xb_, 64, 1))
        odd = jnp.where(low, pltpu.roll(xa, 64, 1), xb_)
        return even, odd

    def spread(u, side):
        v = recv1[u, :, side]
        scratch[side] = v.astype(F32).reshape(256, 128)

    def send_all16(src, by_x, dst, ssem, rsem):
        for d in NEAR:
            t = (s + d) % 16
            tx = t // 4
            tq = t % 4
            pltpu.make_async_remote_copy(
                src.at[tx] if by_x else src.at[tq], dst.at[s], ssem, rsem,
                device_id=(g * 4 + tx, tq), device_id_type=MESH,
            ).start()
        dst[s] = src[x] if by_x else src[q]

    def finish(u):
        hb = orecv[u].astype(F32)
        summed = jnp.concatenate(
            [hb[:, :8].reshape(128, 128), hb[:, 8:].reshape(128, 128)], axis=1
        )
        xn = norm_t(summed).astype(BF16)
        upd = dot(wt[u, 5], xn, NN)
        return (p_t[...] + gate[...] * upd).astype(BF16)

    def emit_sums(cp, oa0, oa1):
        c0 = jnp.where(low, oa0, pltpu.roll(oa1, 64, 1))
        c1 = jnp.where(low, pltpu.roll(oa0, 64, 1), oa1)
        scratch[2, pl.ds(2 * cp, 32, stride=8), :] = c0
        scratch[2, pl.ds(2 * cp + 1, 32, stride=8), :] = c1

    def send_sums(u):
        osend[u] = scratch[2].reshape(16, 16, 128).astype(BF16)
        exchange1(osend.at[u], orecv.at[u], os.at[u], orr.at[u])

    project(0)
    pl.semaphore_wait(barrier, 30)
    exchange1(send1.at[0], recv1.at[0], s1s.at[0], s1r.at[0])
    gate_of(0)
    wait_bytes(recv1.at[0], 15, s1s.at[0], s1r.at[0], False)

    spread(0, 0)
    for cp in range(4):
        even, odd = pairs(0, 0, cp)
        la0[cp] = jnp.concatenate([even, odd], axis=0).astype(BF16)
    for d in (2, 3, 1):
        t = (q + d) % 4
        pltpu.make_async_remote_copy(
            la0, lb0.at[q], l2s.at[0], l2r.at[0], device_id=(row, t), device_id_type=MESH
        ).start()
    lb0[q] = la0[...]
    spread(0, 1)
    for cp in range(4):
        even, odd = pairs(0, 1, cp)
        for j in range(4):
            ra0[j, cp] = jnp.concatenate(
                [even[8 * j : 8 * j + 8], odd[8 * j : 8 * j + 8]], axis=0
            ).astype(BF16)
    send_all16(ra0, False, rb0, r2s.at[0], r2r.at[0])
    wait_bytes(lb0, 3, l2s.at[0], l2r.at[0], False)
    wait_bytes(rb0, 15, r2s.at[0], r2r.at[0], False)

    low64 = iota((64, 128), 1) < 64
    zero = jnp.zeros((64, 128), BF16)
    for cp in range(4):
        a = jnp.concatenate([lb0[k, cp] for k in range(4)], axis=1)
        cols = []
        for k in range(4):
            b = jnp.concatenate([rb0[4 * j + k, cp] for j in range(4)], axis=0)
            cols.append(
                jnp.concatenate([jnp.where(low64, b, zero), jnp.where(low64, zero, b)], axis=0)
            )
        o = dot(a, jnp.concatenate(cols, axis=1), NT)
        emit_sums(cp, o[:32], o[32:])
    send_sums(0)
    wait_bytes(orecv.at[0], 15, os.at[0], orr.at[0], False)
    p_t[...] = finish(0).astype(F32)

    project(1)
    exchange1(send1.at[1], recv1.at[1], s1s.at[1], s1r.at[1])
    gate_of(1)
    wait_bytes(recv1.at[1], 15, s1s.at[1], s1r.at[1], False)

    spread(1, 0)
    pick = onehot(iota((64, 128), 0) == iota((64, 128), 1) % 64)
    for cp in range(4):
        even, odd = pairs(1, 0, cp)
        m = jnp.concatenate([even, odd], axis=0).astype(BF16)
        m2 = jnp.concatenate([jnp.where(low64, m, zero), jnp.where(low64, zero, m)], axis=0)
        t = dot(pick, m2, NT).astype(BF16)
        for k in range(4):
            la1[k, cp] = t[16 * k : 16 * k + 16]
    send_all16(la1, True, lb1, l2s.at[1], l2r.at[1])
    spread(1, 1)
    for cp in range(4):
        even, odd = pairs(1, 1, cp)
        ra1[cp] = jnp.concatenate([even, odd], axis=0).astype(BF16)
    for d in (2, 3, 1):
        t = (x + d) % 4
        pltpu.make_async_remote_copy(
            ra1, rb1.at[x], r2s.at[1], r2r.at[1], device_id=(g * 4 + t, q), device_id_type=MESH
        ).start()
    rb1[x] = ra1[...]
    wait_bytes(lb1, 15, l2s.at[1], l2r.at[1], False)
    wait_bytes(rb1, 3, r2s.at[1], r2r.at[1], False)

    for cp in range(4):
        a = jnp.concatenate(
            [jnp.concatenate([lb1[4 * j + k, cp] for k in range(4)], axis=0) for j in range(4)],
            axis=1,
        )
        rows = []
        for j in range(4):
            b = rb1[j, cp]
            rows += [jnp.where(low64, b, zero), jnp.where(low64, zero, b)]
        o = dot(a, jnp.concatenate(rows, axis=0), NN).reshape(4, 2, 8, 128)
        emit_sums(cp, o[:, 0].reshape(32, 128), o[:, 1].reshape(32, 128))
    send_sums(1)
    wait_bytes(orecv.at[1], 15, os.at[1], orr.at[1], False)
    final = finish(1)
    out[...] = dot(perm, final, NT).astype(BF16).reshape(4, 64, 128)

    for u in range(2):
        wait_bytes(recv1.at[u], 15, s1s.at[u], s1r.at[u], True)
        wait_bytes(orecv.at[u], 15, os.at[u], orr.at[u], True)
    wait_bytes(lb0, 3, l2s.at[0], l2r.at[0], True)
    wait_bytes(rb0, 15, r2s.at[0], r2r.at[0], True)
    wait_bytes(lb1, 15, l2s.at[1], l2r.at[1], True)
    wait_bytes(rb1, 3, r2s.at[1], r2r.at[1], True)


def body(pair, token_mask, w_proj, w_out):
    any_spec = pl.BlockSpec(memory_space=pl.ANY)
    vm = pltpu.VMEM
    dma = pltpu.SemaphoreType.DMA
    return pl.pallas_call(
        kernel,
        out_shape=jax.ShapeDtypeStruct((4, 64, 128), BF16),
        in_specs=[any_spec] * 4,
        out_specs=pl.BlockSpec(memory_space=pltpu.VMEM),
        scratch_shapes=[
            vm((4, 64, 128), BF16),
            vm((1, 256), jnp.int32),
            vm((2, 128, 640), BF16),
            vm((2, 128, 128), BF16),
            vm((2, 6, 128, 128), BF16),
            vm((128, 256), F32),
            vm((128, 256), F32),
            vm((2, 16, 2, 16, 128), BF16),
            vm((2, 16, 2, 16, 128), BF16),
            vm((3, 256, 128), F32),
            vm((4, 64, 128), BF16),
            vm((4, 4, 16, 128), BF16),
            vm((4, 4, 64, 128), BF16),
            vm((16, 4, 16, 128), BF16),
            vm((4, 4, 16, 128), BF16),
            vm((4, 64, 128), BF16),
            vm((16, 4, 16, 128), BF16),
            vm((4, 4, 64, 128), BF16),
            vm((2, 16, 16, 128), BF16),
            vm((2, 16, 16, 128), BF16),
            dma((4,)),
        ]
        + [dma((2,))] * 8,
        compiler_params=pltpu.CompilerParams(
            collective_id=0, has_side_effects=True, vmem_limit_bytes=40 * 2**20
        ),
        name="triangles",
    )(pair, token_mask.reshape(1, 256), w_proj, w_out)


def solution(mesh):
    return jax.shard_map(
        body,
        mesh=mesh,
        in_specs=(P("row", "ka", None), P(), P(), P()),
        out_specs=P("row", "ka", None),
        check_vma=False,
    )
```

```python
import functools

import jax
import jax.numpy as jnp
from jax import lax
from jax.experimental import pallas as pl
from jax.experimental.pallas import tpu as pltpu
from jax.sharding import PartitionSpec as P

EPS = 1e-05
MESH = pl.DeviceIdType.MESH
NEAR = (8, 9, 7, 10, 6, 5, 11, 12, 4, 3, 13, 14, 2, 1, 15)
F32 = jnp.float32
BF16 = jnp.bfloat16
NT = (((1,), (1,)), ((), ()))
NN = (((1,), (0,)), ((), ()))


def dot(a, b, dims):
    return lax.dot_general(a, b, dims, preferred_element_type=F32)


def iota(shape, axis):
    return lax.broadcasted_iota(jnp.int32, shape, axis)


def onehot(cond):
    return jnp.where(cond, 1.0, 0.0).astype(BF16)


def column_of(p):
    return (
        32 * ((p // 4) % 2)
        + 16 * ((p // 2) % 2)
        + 4 * (p // 16)
        + 2 * (p % 2)
        + (p // 8) % 2
    )


def eye(n):
    return onehot(iota((n, n), 0) == iota((n, n), 1))


def norm_t(v):
    mean = jnp.mean(v, axis=0, keepdims=True)
    centered = v - mean
    var = jnp.mean(centered * centered, axis=0, keepdims=True)
    return centered * lax.rsqrt(var + EPS)


def transposed_weight(w, lo):
    return dot(eye(128), w[:, lo : lo + 128], NT).astype(BF16)


def tiles_of(t):
    lo = t[:, :128].reshape(16, 8, 128)
    hi = t[:, 128:].reshape(16, 8, 128)
    return jnp.concatenate([lo, hi], axis=1).astype(BF16)


def kernel(
    pair, mask, wp, wo, out,
    xb, mb, wpb, wob, wt, p_t, gate,
    send1, recv1, scratch, la0, ra0, lb0, rb0, la1, ra1, lb1, rb1, osend, orecv,
    lsem, s1s, s1r, l2s, l2r, cs, cr, r2s, r2r, os, orr,
):
    row = lax.axis_index("row")
    q = lax.axis_index("ka")
    g = row // 4
    x = row % 4
    s = x * 4 + q
    core = q % 2
    mate = q + 1 - 2 * core
    over = (q + 2) % 4

    barrier = pltpu.get_barrier_semaphore()
    for d in NEAR:
        pl.semaphore_signal(
            barrier, inc=1, device_id=(((g + d) % 16) * 4 + x, q), device_id_type=MESH
        )
        t = (s + d) % 16
        pl.semaphore_signal(
            barrier, inc=1, device_id=(g * 4 + t // 4, t % 4), device_id_type=MESH
        )
    loads = [
        pltpu.make_async_copy(a, b, lsem.at[i])
        for i, (a, b) in enumerate(((pair, xb), (mask, mb), (wp, wpb), (wo, wob)))
    ]
    for c in loads:
        c.start()
    for c in loads:
        c.wait()

    for u in range(2):
        for blk in range(5):
            wt[u, blk] = transposed_weight(wpb[u], blk * 128)
        wt[u, 5] = transposed_weight(wob[u], 0)

    n0 = iota((256, 256), 0)
    n1 = iota((256, 256), 1)
    perm_t = onehot(n1 == (n0 // 64) * 64 + column_of(n0 % 64))
    perm = onehot(n0 == (n1 // 64) * 64 + column_of(n1 % 64))
    moved = dot(perm_t, xb[...].reshape(256, 128), NN).astype(BF16)
    p_t[...] = dot(eye(128), moved, NT)
    tokens = jnp.broadcast_to(mb[...].astype(F32), (16, 256)).astype(BF16)
    m_row = dot(tokens, onehot(n0 == 4 * row + n1 // 64), NN)[0:1]
    m_col = dot(tokens, onehot(n0 == 64 * q + column_of(n1 % 64)), NN)[0:1]
    m_pair = m_row * m_col

    def project(u, send):
        normed = norm_t(p_t[...]).astype(BF16)
        ga = dot(wt[u, 0], normed, NN)
        va = dot(wt[u, 1], normed, NN)
        send1[2 * u] = tiles_of(jax.nn.sigmoid(ga) * va * m_pair)
        if send:
            stage1(2 * u)
        gb = dot(wt[u, 2], normed, NN)
        vb = dot(wt[u, 3], normed, NN)
        send1[2 * u + 1] = tiles_of(jax.nn.sigmoid(gb) * vb * m_pair)
        if send:
            stage1(2 * u + 1)

    def gate_of(u):
        normed = norm_t(p_t[...]).astype(BF16)
        gate[...] = jax.nn.sigmoid(dot(wt[u, 4], normed, NN))

    def exchange1(src, dst, ssem, rsem):
        for d in NEAR:
            t = (g + d) % 16
            pltpu.make_async_remote_copy(
                src.at[t], dst.at[g], ssem, rsem, device_id=(t * 4 + x, q), device_id_type=MESH
            ).start()
        dst[g] = src[g]

    def stage1(i):
        exchange1(send1.at[i], recv1.at[i], s1s.at[i], s1r.at[i])

    def stage1_wait(i, send):
        wait_bytes(recv1.at[i], 15, s1s.at[i], s1r.at[i], send)

    def wait_bytes(buf, count, ssem, rsem, send):
        part = buf.at[pl.ds(0, count)]
        c = pltpu.make_async_remote_copy(
            part, part, ssem, rsem, device_id=(g * 4 + (x + 1) % 4, q), device_id_type=MESH
        )
        if send:
            c.wait_send()
        else:
            c.wait_recv()

    low = iota((32, 128), 1) < 64

    def pairs(u, side, cp):
        f = scratch.at[side]
        xa = f[pl.ds(2 * cp, 32, stride=8), :]
        xb_ = f[pl.ds(2 * cp + 1, 32, stride=8), :]
        even = jnp.where(low, xa, pltpu.roll(xb_, 64, 1))
        odd = jnp.where(low, pltpu.roll(xa, 64, 1), xb_)
        return even, odd

    def spread(u, side):
        stage1_wait(2 * u + side, False)
        scratch[side] = recv1[2 * u + side].astype(F32).reshape(256, 128)

    def send_mate(src, dst, ssem, rsem):
        return pltpu.make_async_remote_copy(
            src, dst, ssem, rsem, device_id=(row, mate), device_id_type=MESH
        )

    def send_all16(src, dst, ssem, rsem):
        for d in NEAR:
            t = (s + d) % 16
            tx = t // 4
            tq = t % 4
            pltpu.make_async_remote_copy(
                src.at[tq], dst.at[s], ssem, rsem, device_id=(g * 4 + tx, tq), device_id_type=MESH
            ).start()
        dst[s] = src[q]

    def send_all8(src, dst, ssem, rsem):
        half = x * 2 + q // 2
        for d in (4, 5, 3, 2, 6, 1, 7):
            t = (half + d) % 8
            tx = t // 2
            tq = (t % 2) * 2 + core
            pltpu.make_async_remote_copy(
                src.at[tx], dst.at[half], ssem, rsem, device_id=(g * 4 + tx, tq), device_id_type=MESH
            ).start()
        dst[half] = src[x]

    def finish(u):
        hb = orecv[u].astype(F32)
        summed = jnp.concatenate(
            [hb[:, :8].reshape(128, 128), hb[:, 8:].reshape(128, 128)], axis=1
        )
        xn = norm_t(summed).astype(BF16)
        upd = dot(wt[u, 5], xn, NN)
        return (p_t[...] + gate[...] * upd).astype(BF16)

    def emit_sums(cp, oa0, oa1):
        c0 = jnp.where(low, oa0, pltpu.roll(oa1, 64, 1))
        c1 = jnp.where(low, pltpu.roll(oa0, 64, 1), oa1)
        scratch[2, pl.ds(2 * cp, 32, stride=8), :] = c0
        scratch[2, pl.ds(2 * cp + 1, 32, stride=8), :] = c1

    def send_sums(u):
        osend[u] = scratch[2].reshape(16, 16, 128).astype(BF16)
        exchange1(osend.at[u], orecv.at[u], os.at[u], orr.at[u])

    project(0, False)
    pl.semaphore_wait(barrier, 30)
    stage1(0)
    stage1(1)
    gate_of(0)

    spread(0, 0)
    for cp in range(4):
        even, odd = pairs(0, 0, cp)
        la0[cp] = jnp.concatenate([even, odd], axis=0).astype(BF16)
    across = pltpu.make_async_remote_copy(
        la0, lb0.at[q], l2s.at[0], l2r.at[0], device_id=(row, over), device_id_type=MESH
    )
    across.start()
    to_mate = send_mate(la0, lb0.at[q], cs.at[0], cr.at[0])
    to_mate.start()
    lb0[q] = la0[...]
    spread(0, 1)
    for cp in range(4):
        even, odd = pairs(0, 1, cp)
        for j in range(4):
            ra0[j, cp] = jnp.concatenate(
                [even[8 * j : 8 * j + 8], odd[8 * j : 8 * j + 8]], axis=0
            ).astype(BF16)
    send_all16(ra0, rb0, r2s.at[0], r2r.at[0])
    across.wait_recv()
    passed = send_mate(lb0.at[over], lb0.at[over], cs.at[1], cr.at[1])
    passed.start()
    to_mate.wait_recv()
    wait_bytes(rb0, 15, r2s.at[0], r2r.at[0], False)
    passed.wait_recv()

    low64 = iota((64, 128), 1) < 64
    zero = jnp.zeros((64, 128), BF16)
    for cp in range(4):
        a = jnp.concatenate([lb0[k, cp] for k in range(4)], axis=1)
        cols = []
        for k in range(4):
            b = jnp.concatenate([rb0[4 * j + k, cp] for j in range(4)], axis=0)
            cols.append(
                jnp.concatenate([jnp.where(low64, b, zero), jnp.where(low64, zero, b)], axis=0)
            )
        o = dot(a, jnp.concatenate(cols, axis=1), NT)
        emit_sums(cp, o[:32], o[32:])
    send_sums(0)
    wait_bytes(orecv.at[0], 15, os.at[0], orr.at[0], False)
    p_t[...] = finish(0).astype(F32)

    project(1, True)
    gate_of(1)

    spread(1, 0)
    pick = onehot(iota((64, 128), 0) == iota((64, 128), 1) % 64)
    for cp in range(4):
        even, odd = pairs(1, 0, cp)
        m = jnp.concatenate([even, odd], axis=0).astype(BF16)
        m2 = jnp.concatenate([jnp.where(low64, m, zero), jnp.where(low64, zero, m)], axis=0)
        t = dot(pick, m2, NT).astype(BF16)
        for k in range(4):
            la1[k, cp] = t[16 * k : 16 * k + 16]
    send_all8(la1, lb1.at[core], l2s.at[1], l2r.at[1])
    spread(1, 1)
    for cp in range(4):
        even, odd = pairs(1, 1, cp)
        ra1[cp] = jnp.concatenate([even, odd], axis=0).astype(BF16)
    for d in (2, 3, 1):
        t = (x + d) % 4
        pltpu.make_async_remote_copy(
            ra1, rb1.at[x], r2s.at[1], r2r.at[1], device_id=(g * 4 + t, q), device_id_type=MESH
        ).start()
    rb1[x] = ra1[...]
    wait_bytes(lb1.at[core], 7, l2s.at[1], l2r.at[1], False)
    passed1 = send_mate(lb1.at[core], lb1.at[core], cs.at[2], cr.at[2])
    passed1.start()
    wait_bytes(rb1, 3, r2s.at[1], r2r.at[1], False)
    passed1.wait_recv()

    for cp in range(4):
        a = jnp.concatenate(
            [jnp.concatenate([lb1[k % 2, 2 * j + k // 2, cp] for k in range(4)], axis=0) for j in range(4)],
            axis=1,
        )
        rows = []
        for j in range(4):
            b = rb1[j, cp]
            rows += [jnp.where(low64, b, zero), jnp.where(low64, zero, b)]
        o = dot(a, jnp.concatenate(rows, axis=0), NN).reshape(4, 2, 8, 128)
        emit_sums(cp, o[:, 0].reshape(32, 128), o[:, 1].reshape(32, 128))
    send_sums(1)
    wait_bytes(orecv.at[1], 15, os.at[1], orr.at[1], False)
    final = finish(1)
    out[...] = dot(perm, final, NT).astype(BF16).reshape(4, 64, 128)

    stage1_wait(0, True)
    stage1_wait(1, True)
    across.wait_send()
    to_mate.wait_send()
    passed.wait_send()
    wait_bytes(rb0, 15, r2s.at[0], r2r.at[0], True)
    wait_bytes(orecv.at[0], 15, os.at[0], orr.at[0], True)
    stage1_wait(2, True)
    stage1_wait(3, True)
    wait_bytes(lb1.at[core], 7, l2s.at[1], l2r.at[1], True)
    passed1.wait_send()
    wait_bytes(rb1, 3, r2s.at[1], r2r.at[1], True)
    wait_bytes(orecv.at[1], 15, os.at[1], orr.at[1], True)


def body(pair, token_mask, w_proj, w_out):
    any_spec = pl.BlockSpec(memory_space=pl.ANY)
    vm = pltpu.VMEM
    dma = pltpu.SemaphoreType.DMA
    return pl.pallas_call(
        kernel,
        out_shape=pltpu.VMEM((4, 64, 128), BF16),
        in_specs=[any_spec] * 4,
        out_specs=pl.BlockSpec(memory_space=pltpu.VMEM),
        scratch_shapes=[
            vm((4, 64, 128), BF16),
            vm((1, 256), jnp.int32),
            vm((2, 128, 640), BF16),
            vm((2, 128, 128), BF16),
            vm((2, 6, 128, 128), BF16),
            vm((128, 256), F32),
            vm((128, 256), F32),
            vm((4, 16, 16, 128), BF16),
            vm((4, 16, 16, 128), BF16),
            vm((3, 256, 128), F32),
            vm((4, 64, 128), BF16),
            vm((4, 4, 16, 128), BF16),
            vm((4, 4, 64, 128), BF16),
            vm((16, 4, 16, 128), BF16),
            vm((4, 4, 16, 128), BF16),
            vm((4, 64, 128), BF16),
            vm((2, 8, 4, 16, 128), BF16),
            vm((4, 4, 64, 128), BF16),
            vm((2, 16, 16, 128), BF16),
            vm((2, 16, 16, 128), BF16),
            dma((4,)),
            dma((4,)),
            dma((4,)),
            dma((2,)),
            dma((2,)),
            dma((3,)),
            dma((3,)),
        ]
        + [dma((2,))] * 4,
        compiler_params=pltpu.CompilerParams(
            collective_id=0, has_side_effects=True, vmem_limit_bytes=60 * 2**20
        ),
        name="triangles",
    )(pair, token_mask.reshape(1, 256), w_proj, w_out)


def solution(mesh):
    return jax.shard_map(
        body,
        mesh=mesh,
        in_specs=(P("row", "ka", None), P(), P(), P()),
        out_specs=P("row", "ka", None),
        check_vma=False,
    )
```

```python
import functools

import jax
import jax.numpy as jnp
from jax import lax
from jax.experimental import pallas as pl
from jax.experimental.pallas import tpu as pltpu
from jax.sharding import PartitionSpec as P

EPS = 1e-05
MESH = pl.DeviceIdType.MESH
FAR1 = tuple((dz, e) for dz in (4, 3, 5, 2, 6, 1, 7, 0) for e in (1, 0))[:-1]
FAR2 = (10, 8, 14, 11, 9, 15, 2, 6, 12, 13, 3, 7, 4, 5, 1)
F32 = jnp.float32
BF16 = jnp.bfloat16
NT = (((1,), (1,)), ((), ()))
NN = (((1,), (0,)), ((), ()))


def dot(a, b, dims):
    return lax.dot_general(a, b, dims, preferred_element_type=F32)


def iota(shape, axis):
    return lax.broadcasted_iota(jnp.int32, shape, axis)


def onehot(cond):
    return jnp.where(cond, 1.0, 0.0).astype(BF16)


def column_of(p):
    return 32 * ((p // 4) % 2) + 8 * (p // 16) + 4 * ((p // 2) % 2) + 2 * (p % 2) + (p // 8) % 2


def eye(n):
    return onehot(iota((n, n), 0) == iota((n, n), 1))


def norm_t(v):
    mean = jnp.mean(v, axis=0, keepdims=True)
    centered = v - mean
    var = jnp.mean(centered * centered, axis=0, keepdims=True)
    return centered * lax.rsqrt(var + EPS)


def transposed_weight(w, lo):
    return dot(eye(128), w[:, lo : lo + 128], NT).astype(BF16)


def tiles_of(t):
    lo = t[:, :128].reshape(16, 8, 128)
    hi = t[:, 128:].reshape(16, 8, 128)
    return jnp.concatenate([lo, hi], axis=1).astype(BF16)


def kernel(
    pair, mask, wp, wo, out,
    xb, mb, wpb, wob, wt, p_t, gate,
    send1, recv1, scratch, la0, ra0, lb0, rb0, la1, ra1, lb1, rb1, osend, orecv,
    lsem, s1s, s1r, l2s, l2r, cs, cr, r2s, r2r, os, orr,
):
    row = lax.axis_index("row")
    q = lax.axis_index("ka")
    z = row // 8
    lo = row % 2
    g = z * 2 + lo
    x = (row // 2) % 4
    s = x * 4 + q
    core = q % 2
    mate = q + 1 - 2 * core
    over = (q + 2) % 4

    def row_of(group, v):
        return (group // 2) * 8 + v * 2 + group % 2

    group1 = [((z + dz) % 8) * 2 + (lo + e) % 2 for dz, e in FAR1]
    group2 = []
    for m in FAR2:
        v = ((x // 2 + m // 8) % 2) * 2 + (x + m // 4) % 2
        group2.append((v, ((q // 2 + m // 2) % 2) * 2 + (q + m) % 2))

    barrier = pltpu.get_barrier_semaphore()
    for t in group1:
        pl.semaphore_signal(barrier, inc=1, device_id=(row_of(t, x), q), device_id_type=MESH)
    for v, t in group2:
        pl.semaphore_signal(barrier, inc=1, device_id=(row_of(g, v), t), device_id_type=MESH)
    loads = [
        pltpu.make_async_copy(a, b, lsem.at[i])
        for i, (a, b) in enumerate(((pair, xb), (mask, mb), (wp, wpb), (wo, wob)))
    ]
    for c in loads:
        c.start()
    for c in loads:
        c.wait()

    for u in range(2):
        for blk in range(5):
            wt[u, blk] = transposed_weight(wpb[u], blk * 128)
        wt[u, 5] = transposed_weight(wob[u], 0)

    n0 = iota((256, 256), 0)
    n1 = iota((256, 256), 1)
    perm_t = onehot(n1 == (n0 // 64) * 64 + column_of(n0 % 64))
    perm = onehot(n0 == (n1 // 64) * 64 + column_of(n1 % 64))
    moved = dot(perm_t, xb[...].reshape(256, 128), NN).astype(BF16)
    p_t[...] = dot(eye(128), moved, NT)
    tokens = jnp.broadcast_to(mb[...].astype(F32), (16, 256)).astype(BF16)
    m_row = dot(tokens, onehot(n0 == 4 * row + n1 // 64), NN)[0:1]
    m_col = dot(tokens, onehot(n0 == 64 * q + column_of(n1 % 64)), NN)[0:1]
    m_pair = m_row * m_col

    def project(u):
        normed = norm_t(p_t[...]).astype(BF16)
        ga = dot(wt[u, 0], normed, NN)
        va = dot(wt[u, 1], normed, NN)
        send1[u, :, 0] = tiles_of(jax.nn.sigmoid(ga) * va * m_pair)
        gb = dot(wt[u, 2], normed, NN)
        vb = dot(wt[u, 3], normed, NN)
        send1[u, :, 1] = tiles_of(jax.nn.sigmoid(gb) * vb * m_pair)

    def gate_of(u):
        normed = norm_t(p_t[...]).astype(BF16)
        gate[...] = jax.nn.sigmoid(dot(wt[u, 4], normed, NN))

    def exchange1(src, dst, ssem, rsem):
        for t in group1:
            pltpu.make_async_remote_copy(
                src.at[t], dst.at[g], ssem, rsem, device_id=(row_of(t, x), q), device_id_type=MESH
            ).start()
        dst[g] = src[g]

    def stage1(i):
        exchange1(send1.at[i], recv1.at[i], s1s.at[i], s1r.at[i])

    def stage1_wait(i, send):
        wait_bytes(recv1.at[i], 15, s1s.at[i], s1r.at[i], send)

    def wait_bytes(buf, count, ssem, rsem, send):
        part = buf.at[pl.ds(0, count)]
        c = pltpu.make_async_remote_copy(
            part, part, ssem, rsem, device_id=(row, mate), device_id_type=MESH
        )
        if send:
            c.wait_send()
        else:
            c.wait_recv()

    low = iota((32, 128), 1) < 64

    def pairs(u, side, cp):
        f = scratch.at[side]
        xa = f[pl.ds(2 * cp, 32, stride=8), :]
        xb_ = f[pl.ds(2 * cp + 1, 32, stride=8), :]
        even = jnp.where(low, xa, pltpu.roll(xb_, 64, 1))
        odd = jnp.where(low, pltpu.roll(xa, 64, 1), xb_)
        return even, odd

    def spread(u, side):
        scratch[side] = recv1[u, :, side].astype(F32).reshape(256, 128)

    def send_mate(src, dst, ssem, rsem):
        return pltpu.make_async_remote_copy(
            src, dst, ssem, rsem, device_id=(row, mate), device_id_type=MESH
        )

    def send_all16(src, dst, ssem, rsem):
        for tx, tq in group2:
            pltpu.make_async_remote_copy(
                src.at[tq], dst.at[s], ssem, rsem, device_id=(row_of(g, tx), tq), device_id_type=MESH
            ).start()
        dst[s] = src[q]

    def send_all8(src, dst, ssem, rsem):
        half = x * 2 + q // 2
        for m, (tx, tq) in zip(FAR2, group2):
            if m % 2 == 0:
                pltpu.make_async_remote_copy(
                    src.at[tx], dst.at[half], ssem, rsem,
                    device_id=(row_of(g, tx), tq), device_id_type=MESH,
                ).start()
        dst[half] = src[x]

    def finish(u):
        hb = orecv[u].astype(F32)
        summed = jnp.concatenate(
            [hb[:, :8].reshape(128, 128), hb[:, 8:].reshape(128, 128)], axis=1
        )
        xn = norm_t(summed).astype(BF16)
        upd = dot(wt[u, 5], xn, NN)
        return (p_t[...] + gate[...] * upd).astype(BF16)

    def emit_sums(cp, oa0, oa1):
        c0 = jnp.where(low, oa0, pltpu.roll(oa1, 64, 1))
        c1 = jnp.where(low, pltpu.roll(oa0, 64, 1), oa1)
        scratch[2, pl.ds(2 * cp, 32, stride=8), :] = c0
        scratch[2, pl.ds(2 * cp + 1, 32, stride=8), :] = c1

    def send_sums(u):
        osend[u] = scratch[2].reshape(16, 16, 128).astype(BF16)
        exchange1(osend.at[u], orecv.at[u], os.at[u], orr.at[u])

    project(0)
    pl.semaphore_wait(barrier, 30)
    stage1(0)
    gate_of(0)
    stage1_wait(0, False)

    spread(0, 0)
    for cp in range(4):
        even, odd = pairs(0, 0, cp)
        la0[cp] = jnp.concatenate([even, odd], axis=0).astype(BF16)
    across = pltpu.make_async_remote_copy(
        la0, lb0.at[q], l2s.at[0], l2r.at[0], device_id=(row, over), device_id_type=MESH
    )
    across.start()
    to_mate = send_mate(la0, lb0.at[q], cs.at[0], cr.at[0])
    to_mate.start()
    lb0[q] = la0[...]
    spread(0, 1)
    for cp in range(4):
        even, odd = pairs(0, 1, cp)
        for j in range(4):
            ra0[j, cp] = jnp.concatenate(
                [even[8 * j : 8 * j + 8], odd[8 * j : 8 * j + 8]], axis=0
            ).astype(BF16)
    send_all16(ra0, rb0, r2s.at[0], r2r.at[0])
    across.wait_recv()
    passed = send_mate(lb0.at[over], lb0.at[over], cs.at[1], cr.at[1])
    passed.start()
    to_mate.wait_recv()
    wait_bytes(rb0, 15, r2s.at[0], r2r.at[0], False)
    passed.wait_recv()

    low64 = iota((64, 128), 1) < 64
    zero = jnp.zeros((64, 128), BF16)
    for cp in range(4):
        a = jnp.concatenate([lb0[k, cp] for k in range(4)], axis=1)
        cols = []
        for k in range(4):
            b = jnp.concatenate([rb0[4 * j + k, cp] for j in range(4)], axis=0)
            cols.append(
                jnp.concatenate([jnp.where(low64, b, zero), jnp.where(low64, zero, b)], axis=0)
            )
        o = dot(a, jnp.concatenate(cols, axis=1), NT)
        emit_sums(cp, o[:32], o[32:])
    send_sums(0)
    wait_bytes(orecv.at[0], 15, os.at[0], orr.at[0], False)
    p_t[...] = finish(0).astype(F32)

    project(1)
    stage1(1)
    gate_of(1)
    stage1_wait(1, False)
    spread(1, 0)
    pick = onehot(iota((64, 128), 0) == iota((64, 128), 1) % 64)
    for cp in range(4):
        even, odd = pairs(1, 0, cp)
        m = jnp.concatenate([even, odd], axis=0).astype(BF16)
        m2 = jnp.concatenate([jnp.where(low64, m, zero), jnp.where(low64, zero, m)], axis=0)
        t = dot(pick, m2, NT).astype(BF16)
        for k in range(4):
            la1[k, cp] = t[16 * k : 16 * k + 16]
    send_all8(la1, lb1.at[core], l2s.at[1], l2r.at[1])
    spread(1, 1)
    for cp in range(4):
        even, odd = pairs(1, 1, cp)
        ra1[cp] = jnp.concatenate([even, odd], axis=0).astype(BF16)
    for m, (t, _) in zip(FAR2, group2):
        if m % 4 == 0:
            pltpu.make_async_remote_copy(
                ra1, rb1.at[x], r2s.at[1], r2r.at[1],
                device_id=(row_of(g, t), q), device_id_type=MESH,
            ).start()
    rb1[x] = ra1[...]
    wait_bytes(lb1.at[core], 7, l2s.at[1], l2r.at[1], False)
    passed1 = send_mate(lb1.at[core], lb1.at[core], cs.at[2], cr.at[2])
    passed1.start()
    wait_bytes(rb1, 3, r2s.at[1], r2r.at[1], False)
    passed1.wait_recv()

    for cp in range(4):
        a = jnp.concatenate(
            [jnp.concatenate([lb1[k % 2, 2 * j + k // 2, cp] for k in range(4)], axis=0) for j in range(4)],
            axis=1,
        )
        rows = []
        for j in range(4):
            b = rb1[j, cp]
            rows += [jnp.where(low64, b, zero), jnp.where(low64, zero, b)]
        o = dot(a, jnp.concatenate(rows, axis=0), NN).reshape(4, 2, 8, 128)
        emit_sums(cp, o[:, 0].reshape(32, 128), o[:, 1].reshape(32, 128))
    send_sums(1)
    wait_bytes(orecv.at[1], 15, os.at[1], orr.at[1], False)
    final = finish(1)
    out[...] = dot(perm, final, NT).astype(BF16).reshape(4, 64, 128)

    stage1_wait(0, True)
    across.wait_send()
    to_mate.wait_send()
    passed.wait_send()
    wait_bytes(rb0, 15, r2s.at[0], r2r.at[0], True)
    wait_bytes(orecv.at[0], 15, os.at[0], orr.at[0], True)
    stage1_wait(1, True)
    wait_bytes(lb1.at[core], 7, l2s.at[1], l2r.at[1], True)
    passed1.wait_send()
    wait_bytes(rb1, 3, r2s.at[1], r2r.at[1], True)
    wait_bytes(orecv.at[1], 15, os.at[1], orr.at[1], True)


def body(pair, token_mask, w_proj, w_out):
    any_spec = pl.BlockSpec(memory_space=pl.ANY)
    vm = pltpu.VMEM
    dma = pltpu.SemaphoreType.DMA
    return pl.pallas_call(
        kernel,
        out_shape=pltpu.VMEM((4, 64, 128), BF16),
        in_specs=[any_spec] * 4,
        out_specs=pl.BlockSpec(memory_space=pltpu.VMEM),
        scratch_shapes=[
            vm((4, 64, 128), BF16),
            vm((1, 256), jnp.int32),
            vm((2, 128, 640), BF16),
            vm((2, 128, 128), BF16),
            vm((2, 6, 128, 128), BF16),
            vm((128, 256), F32),
            vm((128, 256), F32),
            vm((2, 16, 2, 16, 128), BF16),
            vm((2, 16, 2, 16, 128), BF16),
            vm((3, 256, 128), F32),
            vm((4, 64, 128), BF16),
            vm((4, 4, 16, 128), BF16),
            vm((4, 4, 64, 128), BF16),
            vm((16, 4, 16, 128), BF16),
            vm((4, 4, 16, 128), BF16),
            vm((4, 64, 128), BF16),
            vm((2, 8, 4, 16, 128), BF16),
            vm((4, 4, 64, 128), BF16),
            vm((2, 16, 16, 128), BF16),
            vm((2, 16, 16, 128), BF16),
            dma((4,)),
            dma((2,)),
            dma((2,)),
            dma((2,)),
            dma((2,)),
            dma((3,)),
            dma((3,)),
        ]
        + [dma((2,))] * 4,
        compiler_params=pltpu.CompilerParams(
            collective_id=0, has_side_effects=True, vmem_limit_bytes=60 * 2**20
        ),
        name="triangles",
    )(pair, token_mask.reshape(1, 256), w_proj, w_out)


def solution(mesh):
    return jax.shard_map(
        body,
        mesh=mesh,
        in_specs=(P("row", "ka", None), P(), P(), P()),
        out_specs=P("row", "ka", None),
        check_vma=False,
    )
```

```python
import functools

import jax
import jax.numpy as jnp
from jax import lax
from jax.experimental import pallas as pl
from jax.experimental.pallas import tpu as pltpu
from jax.sharding import PartitionSpec as P

EPS = 1e-05
PE, PH, PL = 1, 4, 2
MESH = pl.DeviceIdType.MESH
FAR1 = tuple((dz, e) for dz in (4, 3, 5, 2, 6, 1, 7, 0) for e in (1, 0))[:-1]
FAR2 = (12, 13, 14, 15, 6, 7, 8, 9, 4, 5, 10, 11, 2, 3, 1)
F32 = jnp.float32
BF16 = jnp.bfloat16
NT = (((1,), (1,)), ((), ()))
NN = (((1,), (0,)), ((), ()))


def dot(a, b, dims):
    return lax.dot_general(a, b, dims, preferred_element_type=F32)


def iota(shape, axis):
    return lax.broadcasted_iota(jnp.int32, shape, axis)


def onehot(cond):
    return jnp.where(cond, 1.0, 0.0).astype(BF16)


def column_of(p):
    v = PH * (p // 32) + PL * ((p // 16) % 2) + PE * ((p // 2) % 2)
    return 32 * ((p // 4) % 2) + 4 * v + 2 * (p % 2) + (p // 8) % 2


def eye(n):
    return onehot(iota((n, n), 0) == iota((n, n), 1))


def norm_t(v):
    mean = jnp.mean(v, axis=0, keepdims=True)
    centered = v - mean
    var = jnp.mean(centered * centered, axis=0, keepdims=True)
    return centered * lax.rsqrt(var + EPS)


def transposed_weight(w, lo):
    return dot(eye(128), w[:, lo : lo + 128], NT).astype(BF16)


def tiles_of(t):
    lo = t[:, :128].reshape(16, 8, 128)
    hi = t[:, 128:].reshape(16, 8, 128)
    return jnp.concatenate([lo, hi], axis=1).astype(BF16)


def kernel(
    pair, mask, wp, wo, out,
    xb, mb, wpb, wob, wt, p_t, gate,
    send1, recv1, scratch, la0, ra0, lb0, rb0, la1, ra1, lb1, rb1, osend, orecv,
    lsem, s1s, s1r, l2s, l2r, l1s, l1r, cs, cr, r2s, r2r, os, orr,
):
    row = lax.axis_index("row")
    q = lax.axis_index("ka")
    z = row // 8
    lo = (row // PE) % 2
    g = z * 2 + lo
    x = ((row // PH) % 2) * 2 + (row // PL) % 2
    s = x * 4 + q
    core = q % 2
    mate = q + 1 - 2 * core
    over = (q + 2) % 4
    side = q // 2

    def row_of(group, v):
        return (group // 2) * 8 + (v // 2) * PH + (v % 2) * PL + (group % 2) * PE

    group1 = [((z + dz) % 8) * 2 + (lo + e) % 2 for dz, e in FAR1]
    group2 = []
    for m in FAR2:
        v = ((x // 2 + m // 8) % 2) * 2 + (x + m // 4) % 2
        group2.append((v, ((q // 2 + m // 2) % 2) * 2 + (q + m) % 2))

    barrier = pltpu.get_barrier_semaphore()
    for t in group1:
        pl.semaphore_signal(barrier, inc=1, device_id=(row_of(t, x), q), device_id_type=MESH)
    for v, t in group2:
        pl.semaphore_signal(barrier, inc=1, device_id=(row_of(g, v), t), device_id_type=MESH)
    loads = [
        pltpu.make_async_copy(a, b, lsem.at[i])
        for i, (a, b) in enumerate(((pair, xb), (mask, mb), (wp, wpb), (wo, wob)))
    ]
    for c in loads:
        c.start()
    for c in loads:
        c.wait()

    for u in range(2):
        for blk in range(5):
            wt[u, blk] = transposed_weight(wpb[u], blk * 128)
        wt[u, 5] = transposed_weight(wob[u], 0)

    n0 = iota((256, 256), 0)
    n1 = iota((256, 256), 1)
    perm_t = onehot(n1 == (n0 // 64) * 64 + column_of(n0 % 64))
    perm = onehot(n0 == (n1 // 64) * 64 + column_of(n1 % 64))
    moved = dot(perm_t, xb[...].reshape(256, 128), NN).astype(BF16)
    p_t[...] = dot(eye(128), moved, NT)
    tokens = jnp.broadcast_to(mb[...].astype(F32), (16, 256)).astype(BF16)
    m_row = dot(tokens, onehot(n0 == 4 * row + n1 // 64), NN)[0:1]
    m_col = dot(tokens, onehot(n0 == 64 * q + column_of(n1 % 64)), NN)[0:1]
    m_pair = m_row * m_col

    def project(u):
        normed = norm_t(p_t[...]).astype(BF16)
        ga = dot(wt[u, 0], normed, NN)
        va = dot(wt[u, 1], normed, NN)
        send1[u, :, 0] = tiles_of(jax.nn.sigmoid(ga) * va * m_pair)
        gb = dot(wt[u, 2], normed, NN)
        vb = dot(wt[u, 3], normed, NN)
        send1[u, :, 1] = tiles_of(jax.nn.sigmoid(gb) * vb * m_pair)

    def gate_of(u):
        normed = norm_t(p_t[...]).astype(BF16)
        gate[...] = jax.nn.sigmoid(dot(wt[u, 4], normed, NN))

    def exchange1(src, dst, ssem, rsem):
        for t in group1:
            pltpu.make_async_remote_copy(
                src.at[t], dst.at[g], ssem, rsem, device_id=(row_of(t, x), q), device_id_type=MESH
            ).start()
        dst[g] = src[g]

    def stage1(i):
        exchange1(send1.at[i], recv1.at[i], s1s.at[i], s1r.at[i])

    def stage1_wait(i, send):
        wait_bytes(recv1.at[i], 15, s1s.at[i], s1r.at[i], send)

    def wait_bytes(buf, count, ssem, rsem, send):
        part = buf.at[pl.ds(0, count)]
        c = pltpu.make_async_remote_copy(
            part, part, ssem, rsem, device_id=(row, mate), device_id_type=MESH
        )
        if send:
            c.wait_send()
        else:
            c.wait_recv()

    low = iota((32, 128), 1) < 64

    def pairs(u, side, cp):
        f = scratch.at[side]
        xa = f[pl.ds(2 * cp, 32, stride=8), :]
        xb_ = f[pl.ds(2 * cp + 1, 32, stride=8), :]
        even = jnp.where(low, xa, pltpu.roll(xb_, 64, 1))
        odd = jnp.where(low, pltpu.roll(xa, 64, 1), xb_)
        return even, odd

    def spread(u, side):
        scratch[side] = recv1[u, :, side].astype(F32).reshape(256, 128)

    def send_mate(src, dst, ssem, rsem):
        return pltpu.make_async_remote_copy(
            src, dst, ssem, rsem, device_id=(row, mate), device_id_type=MESH
        )

    def send_all16(src, dst, ssem, rsem):
        for tx, tq in group2:
            pltpu.make_async_remote_copy(
                src.at[tq], dst.at[s], ssem, rsem, device_id=(row_of(g, tx), tq), device_id_type=MESH
            ).start()
        dst[s] = src[q]

    def send_left1():
        for v in range(4):
            for y in range(2):
                copy = pltpu.make_async_remote_copy(
                    la1.at[v], lb1.at[core, side, x], l1s, l1r.at[side],
                    device_id=(row_of(g, v), y * 2 + core), device_id_type=MESH,
                )
                pl.when((x != v) | (side != y))(copy.start)
        pltpu.make_async_copy(la1.at[x], lb1.at[core, side, x], l1r.at[side]).start()

    def send_right1():
        for v in range(4):
            copy = pltpu.make_async_remote_copy(
                ra1, rb1.at[x], r2s.at[1], r2r.at[1],
                device_id=(row_of(g, v), q), device_id_type=MESH,
            )
            pl.when(x != v)(copy.start)

    def send_sums_half(c):
        part = sums_rows(c)
        osend[1, 8 * c : 8 * c + 8] = part.reshape(8, 16, 128).astype(BF16)

        def out(t):
            return pltpu.make_async_remote_copy(
                osend.at[1, t], orecv.at[1, g], os.at[1], orr.at[1],
                device_id=(row_of(t, x), q), device_id_type=MESH,
            )

        for i in (4, 5, 3, 2, 6, 7, 1):
            out(8 * c + (g + i) % 8).start()

        @pl.when(g // 8 != c)
        def _():
            out(8 * c + g % 8).start()

        @pl.when(g // 8 == c)
        def _():
            orecv[1, g] = osend[1, g]

    def sums_rows(c):
        return scratch[2, 128 * c : 128 * c + 128]

    def finish(u):
        hb = orecv[u].astype(F32)
        summed = jnp.concatenate(
            [hb[:, :8].reshape(128, 128), hb[:, 8:].reshape(128, 128)], axis=1
        )
        xn = norm_t(summed).astype(BF16)
        upd = dot(wt[u, 5], xn, NN)
        return (p_t[...] + gate[...] * upd).astype(BF16)

    def emit_sums(cp, oa0, oa1, base=0):
        n = oa0.shape[0]
        low = iota((n, 128), 1) < 64
        c0 = jnp.where(low, oa0, pltpu.roll(oa1, 64, 1))
        c1 = jnp.where(low, pltpu.roll(oa0, 64, 1), oa1)
        scratch[2, pl.ds(base + 2 * cp, n, stride=8), :] = c0
        scratch[2, pl.ds(base + 2 * cp + 1, n, stride=8), :] = c1

    def send_sums(u):
        osend[u] = scratch[2].reshape(16, 16, 128).astype(BF16)
        exchange1(osend.at[u], orecv.at[u], os.at[u], orr.at[u])

    project(0)
    pl.semaphore_wait(barrier, 30)
    stage1(0)
    gate_of(0)
    stage1_wait(0, False)

    spread(0, 0)
    for cp in range(4):
        even, odd = pairs(0, 0, cp)
        la0[cp] = jnp.concatenate([even, odd], axis=0).astype(BF16)
    across = pltpu.make_async_remote_copy(
        la0, lb0.at[q], l2s.at[0], l2r.at[0], device_id=(row, over), device_id_type=MESH
    )
    across.start()
    to_mate = send_mate(la0, lb0.at[q], cs.at[0], cr.at[0])
    to_mate.start()
    lb0[q] = la0[...]
    spread(0, 1)
    for cp in range(4):
        even, odd = pairs(0, 1, cp)
        for j in range(4):
            ra0[j, cp] = jnp.concatenate(
                [even[8 * j : 8 * j + 8], odd[8 * j : 8 * j + 8]], axis=0
            ).astype(BF16)
    send_all16(ra0, rb0, r2s.at[0], r2r.at[0])
    across.wait_recv()
    passed = send_mate(lb0.at[over], lb0.at[over], cs.at[1], cr.at[1])
    passed.start()
    to_mate.wait_recv()
    wait_bytes(rb0, 15, r2s.at[0], r2r.at[0], False)
    passed.wait_recv()

    low64 = iota((64, 128), 1) < 64
    zero = jnp.zeros((64, 128), BF16)
    for cp in range(4):
        a = jnp.concatenate([lb0[k, cp] for k in range(4)], axis=1)
        cols = []
        for k in range(4):
            b = jnp.concatenate([rb0[4 * j + k, cp] for j in range(4)], axis=0)
            cols.append(
                jnp.concatenate([jnp.where(low64, b, zero), jnp.where(low64, zero, b)], axis=0)
            )
        o = dot(a, jnp.concatenate(cols, axis=1), NT)
        emit_sums(cp, o[:32], o[32:])
    send_sums(0)
    wait_bytes(orecv.at[0], 15, os.at[0], orr.at[0], False)
    p_t[...] = finish(0).astype(F32)

    project(1)
    stage1(1)
    gate_of(1)
    stage1_wait(1, False)
    spread(1, 0)
    pick = onehot(iota((64, 128), 0) == iota((64, 128), 1) % 64)
    for cp in range(4):
        even, odd = pairs(1, 0, cp)
        m = jnp.concatenate([even, odd], axis=0).astype(BF16)
        m2 = jnp.concatenate([jnp.where(low64, m, zero), jnp.where(low64, zero, m)], axis=0)
        t = dot(pick, m2, NT).astype(BF16)
        for k in range(4):
            la1[k, cp] = t[16 * k : 16 * k + 16]
    @pl.when(side == 0)
    def _():
        send_left1()

    spread(1, 1)
    for cp in range(4):
        even, odd = pairs(1, 1, cp)
        ra1[cp] = jnp.concatenate([even, odd], axis=0).astype(BF16)
    send_right1()

    @pl.when(side == 1)
    def _():
        send_left1()

    rb1[x] = ra1[...]
    passed1 = []
    for c in range(2):
        got = lb1.at[core, c]
        pltpu.make_async_remote_copy(
            got, got, l1s, l1r.at[c], device_id=(row, mate), device_id_type=MESH
        ).wait_recv()
        passed1.append(send_mate(got, got, cs.at[2 + c], cr.at[2 + c]))
        passed1[c].start()
        if c == 0:
            wait_bytes(rb1, 3, r2s.at[1], r2r.at[1], False)
        passed1[c].wait_recv()
        for cp in range(4):
            a = jnp.concatenate(
                [jnp.concatenate([lb1[k, c, j, cp] for k in range(2)], axis=0) for j in range(4)],
                axis=1,
            )
            rows = []
            for j in range(4):
                b = rb1[j, cp]
                rows += [jnp.where(low64, b, zero), jnp.where(low64, zero, b)]
            o = dot(a, jnp.concatenate(rows, axis=0), NN).reshape(2, 2, 8, 128)
            emit_sums(cp, o[:, 0].reshape(16, 128), o[:, 1].reshape(16, 128), 128 * c)
        send_sums_half(c)
    wait_bytes(orecv.at[1], 15, os.at[1], orr.at[1], False)
    final = finish(1)
    out[...] = dot(perm, final, NT).astype(BF16).reshape(4, 64, 128)

    stage1_wait(0, True)
    across.wait_send()
    to_mate.wait_send()
    passed.wait_send()
    wait_bytes(rb0, 15, r2s.at[0], r2r.at[0], True)
    wait_bytes(orecv.at[0], 15, os.at[0], orr.at[0], True)
    stage1_wait(1, True)
    wait_bytes(rb0, 7, l1s, l1r.at[0], True)
    for c in passed1:
        c.wait_send()
    wait_bytes(rb1, 3, r2s.at[1], r2r.at[1], True)
    wait_bytes(orecv.at[1], 15, os.at[1], orr.at[1], True)


def body(pair, token_mask, w_proj, w_out):
    any_spec = pl.BlockSpec(memory_space=pl.ANY)
    vm = pltpu.VMEM
    dma = pltpu.SemaphoreType.DMA
    return pl.pallas_call(
        kernel,
        out_shape=pltpu.VMEM((4, 64, 128), BF16),
        in_specs=[any_spec] * 4,
        out_specs=pl.BlockSpec(memory_space=pltpu.VMEM),
        scratch_shapes=[
            vm((4, 64, 128), BF16),
            vm((1, 256), jnp.int32),
            vm((2, 128, 640), BF16),
            vm((2, 128, 128), BF16),
            vm((2, 6, 128, 128), BF16),
            vm((128, 256), F32),
            vm((128, 256), F32),
            vm((2, 16, 2, 16, 128), BF16),
            vm((2, 16, 2, 16, 128), BF16),
            vm((3, 256, 128), F32),
            vm((4, 64, 128), BF16),
            vm((4, 4, 16, 128), BF16),
            vm((4, 4, 64, 128), BF16),
            vm((16, 4, 16, 128), BF16),
            vm((4, 4, 16, 128), BF16),
            vm((4, 64, 128), BF16),
            vm((2, 2, 4, 4, 16, 128), BF16),
            vm((4, 4, 64, 128), BF16),
            vm((2, 16, 16, 128), BF16),
            vm((2, 16, 16, 128), BF16),
            dma((4,)),
            dma((2,)),
            dma((2,)),
            dma((1,)),
            dma((1,)),
            dma,
            dma((2,)),
            dma((4,)),
            dma((4,)),
        ]
        + [dma((2,))] * 4,
        compiler_params=pltpu.CompilerParams(
            collective_id=0, has_side_effects=True, vmem_limit_bytes=60 * 2**20
        ),
        name="triangles",
    )(pair, token_mask.reshape(1, 256), w_proj, w_out)


def solution(mesh):
    return jax.shard_map(
        body,
        mesh=mesh,
        in_specs=(P("row", "ka", None), P(), P(), P()),
        out_specs=P("row", "ka", None),
        check_vma=False,
    )
```

```python
import functools

import jax
import jax.numpy as jnp
from jax import lax
from jax.experimental import pallas as pl
from jax.experimental.pallas import tpu as pltpu
from jax.sharding import PartitionSpec as P

EPS = 1e-05
PE, PH, PL = 1, 4, 2
MESH = pl.DeviceIdType.MESH
FAR1 = tuple((dz, e) for dz in (4, 3, 5, 2, 6, 1, 7, 0) for e in (1, 0))[:-1]
FAR2 = (12, 13, 14, 15, 6, 7, 8, 9, 4, 5, 10, 11, 2, 3, 1)
F32 = jnp.float32
BF16 = jnp.bfloat16
NT = (((1,), (1,)), ((), ()))
NN = (((1,), (0,)), ((), ()))


def dot(a, b, dims):
    return lax.dot_general(a, b, dims, preferred_element_type=F32)


def iota(shape, axis):
    return lax.broadcasted_iota(jnp.int32, shape, axis)


def onehot(cond):
    return jnp.where(cond, 1.0, 0.0).astype(BF16)


def column_of(p):
    v = PH * (p // 32) + PL * ((p // 16) % 2) + PE * ((p // 2) % 2)
    return 32 * ((p // 4) % 2) + 4 * v + 2 * (p % 2) + (p // 8) % 2


def eye(n):
    return onehot(iota((n, n), 0) == iota((n, n), 1))


def norm_t(v):
    mean = jnp.mean(v, axis=0, keepdims=True)
    centered = v - mean
    var = jnp.mean(centered * centered, axis=0, keepdims=True)
    return centered * lax.rsqrt(var + EPS)


def transposed_weight(w, lo):
    return dot(eye(128), w[:, lo : lo + 128], NT).astype(BF16)


def tiles_of(t):
    lo = t[:, :128].reshape(16, 8, 128)
    hi = t[:, 128:].reshape(16, 8, 128)
    return jnp.concatenate([lo, hi], axis=1).astype(BF16)


def kernel(
    pair, mask, wp, wo, out,
    xb, mb, wpb, wob, wt, p_t, gate, perm,
    send1, recv1, scratch, la0, ra0, lb0, rb0, la1, rdir, lb1, rb1, osend, orecv,
    lsem, s1s, s1r, rds, rdr, l2s, l2r, l1s, l1r, cs, cr, r2s, r2r, os, orr,
):
    row = lax.axis_index("row")
    q = lax.axis_index("ka")
    z = row // 8
    lo = (row // PE) % 2
    g = z * 2 + lo
    x = ((row // PH) % 2) * 2 + (row // PL) % 2
    s = x * 4 + q
    core = q % 2
    mate = q + 1 - 2 * core
    over = (q + 2) % 4
    side = q // 2

    def row_of(group, v):
        return (group // 2) * 8 + (v // 2) * PH + (v % 2) * PL + (group % 2) * PE

    classes = [((x // 2 + f // 2) % 2) * 2 + (x + f) % 2 for f in range(4)]
    group1 = [((z + dz) % 8) * 2 + (lo + e) % 2 for dz, e in FAR1]
    group2 = []
    for m in FAR2:
        v = ((x // 2 + m // 8) % 2) * 2 + (x + m // 4) % 2
        group2.append((v, ((q // 2 + m // 2) % 2) * 2 + (q + m) % 2))

    barrier = pltpu.get_barrier_semaphore()
    for t in group1:
        pl.semaphore_signal(barrier, inc=1, device_id=(row_of(t, x), q), device_id_type=MESH)
    for v, t in group2:
        pl.semaphore_signal(barrier, inc=1, device_id=(row_of(g, v), t), device_id_type=MESH)
    loads = [
        pltpu.make_async_copy(a, b, lsem.at[i])
        for i, (a, b) in enumerate(((pair, xb), (mask, mb), (wp, wpb), (wo, wob)))
    ]
    for c in loads:
        c.start()
    for c in loads:
        c.wait()

    for blk in range(4):
        wt[0, blk] = transposed_weight(wpb[0], blk * 128)

    n0 = iota((256, 256), 0)
    n1 = iota((256, 256), 1)
    perm_t = onehot(n1 == (n0 // 64) * 64 + column_of(n0 % 64))
    moved = dot(perm_t, xb[...].reshape(256, 128), NN).astype(BF16)
    p_t[...] = dot(eye(128), moved, NT)
    tokens = jnp.broadcast_to(mb[...].astype(F32), (16, 256)).astype(BF16)
    m_row = dot(tokens, onehot(n0 == 4 * row + n1 // 64), NN)[0:1]
    m_col = dot(tokens, onehot(n0 == 64 * q + column_of(n1 % 64)), NN)[0:1]
    m_pair = m_row * m_col

    def project(u):
        normed = norm_t(p_t[...]).astype(BF16)
        ga = dot(wt[u, 0], normed, NN)
        va = dot(wt[u, 1], normed, NN)
        send1[u, :, 0] = tiles_of(jax.nn.sigmoid(ga) * va * m_pair)
        gb = dot(wt[u, 2], normed, NN)
        vb = dot(wt[u, 3], normed, NN)
        send1[u, :, 1] = tiles_of(jax.nn.sigmoid(gb) * vb * m_pair)

    def gate_of(u):
        normed = norm_t(p_t[...]).astype(BF16)
        gate[...] = jax.nn.sigmoid(dot(wt[u, 4], normed, NN))

    def exchange1(src, dst, ssem, rsem):
        for t in group1:
            pltpu.make_async_remote_copy(
                src.at[t], dst.at[g], ssem, rsem, device_id=(row_of(t, x), q), device_id_type=MESH
            ).start()
        dst[g] = src[g]

    def stage1(i):
        exchange1(send1.at[i], recv1.at[i], s1s.at[i], s1r.at[i])

    def stage1_left():
        for t in group1:
            pltpu.make_async_remote_copy(
                send1.at[1, t, 0], recv1.at[1, g, 0], s1s.at[1], s1r.at[1],
                device_id=(row_of(t, x), q), device_id_type=MESH,
            ).start()
        recv1[1, g, 0] = send1[1, g, 0]

    def direct_right():
        for d in (3, 2, 1, 0):
            v = classes[d]

            def step(i, carry):
                t = (g + 8 + ((i + 1) // 2) * (1 - 2 * (i % 2))) % 16
                pltpu.make_async_remote_copy(
                    send1.at[1, t, 1], rdir.at[x, g], rds, rdr.at[x],
                    device_id=(row_of(t, v), q), device_id_type=MESH,
                ).start()
                return carry

            lax.fori_loop(0, 15 if d == 0 else 16, step, 0)
        rdir[x, g] = send1[1, g, 1]

    def right_from(d):
        v = classes[d]
        n = 15 if d == 0 else 16
        part = osend.at[0, pl.ds(0, n)]
        pltpu.make_async_remote_copy(
            part, part, rds, rdr.at[v], device_id=(row, mate), device_id_type=MESH
        ).wait_recv()
        scratch[1] = rdir[v].astype(F32).reshape(256, 128)
        for cp in range(4):
            even, odd = pairs(1, 1, cp)
            rb1[v, cp] = jnp.concatenate([even, odd], axis=0).astype(BF16)

    def stage1_wait(i, send):
        wait_bytes(recv1.at[i], 15, s1s.at[i], s1r.at[i], send)

    def wait_bytes(buf, count, ssem, rsem, send):
        part = buf.at[pl.ds(0, count)]
        c = pltpu.make_async_remote_copy(
            part, part, ssem, rsem, device_id=(row, mate), device_id_type=MESH
        )
        if send:
            c.wait_send()
        else:
            c.wait_recv()

    low = iota((32, 128), 1) < 64

    def pairs(u, side, cp):
        f = scratch.at[side]
        xa = f[pl.ds(2 * cp, 32, stride=8), :]
        xb_ = f[pl.ds(2 * cp + 1, 32, stride=8), :]
        even = jnp.where(low, xa, pltpu.roll(xb_, 64, 1))
        odd = jnp.where(low, pltpu.roll(xa, 64, 1), xb_)
        return even, odd

    def spread(u, side):
        scratch[side] = recv1[u, :, side].astype(F32).reshape(256, 128)

    def send_mate(src, dst, ssem, rsem):
        return pltpu.make_async_remote_copy(
            src, dst, ssem, rsem, device_id=(row, mate), device_id_type=MESH
        )

    def send_all16(src, dst, ssem, rsem):
        for tx, tq in group2:
            pltpu.make_async_remote_copy(
                src.at[tq], dst.at[s], ssem, rsem, device_id=(row_of(g, tx), tq), device_id_type=MESH
            ).start()
        dst[s] = src[q]

    def send_left1():
        for v in range(4):
            for y in range(2):
                copy = pltpu.make_async_remote_copy(
                    la1.at[v], lb1.at[core, side, x], l1s, l1r.at[side],
                    device_id=(row_of(g, v), y * 2 + core), device_id_type=MESH,
                )
                pl.when((x != v) | (side != y))(copy.start)
        pltpu.make_async_copy(la1.at[x], lb1.at[core, side, x], l1r.at[side]).start()

    def send_sums_half(c):
        part = sums_rows(c)
        osend[1, 8 * c : 8 * c + 8] = part.reshape(8, 16, 128).astype(BF16)

        def out(t):
            return pltpu.make_async_remote_copy(
                osend.at[1, t], orecv.at[1, g], os.at[1], orr.at[1],
                device_id=(row_of(t, x), q), device_id_type=MESH,
            )

        for i in (4, 5, 3, 2, 6, 7, 1):
            out(8 * c + (g + i) % 8).start()

        @pl.when(g // 8 != c)
        def _():
            out(8 * c + g % 8).start()

        @pl.when(g // 8 == c)
        def _():
            orecv[1, g] = osend[1, g]

    def sums_rows(c):
        return scratch[2, 128 * c : 128 * c + 128]

    def finish(u):
        hb = orecv[u].astype(F32)
        summed = jnp.concatenate(
            [hb[:, :8].reshape(128, 128), hb[:, 8:].reshape(128, 128)], axis=1
        )
        xn = norm_t(summed).astype(BF16)
        upd = dot(wt[u, 5], xn, NN)
        return (p_t[...] + gate[...] * upd).astype(BF16)

    def emit_sums(cp, oa0, oa1, base=0):
        n = oa0.shape[0]
        low = iota((n, 128), 1) < 64
        c0 = jnp.where(low, oa0, pltpu.roll(oa1, 64, 1))
        c1 = jnp.where(low, pltpu.roll(oa0, 64, 1), oa1)
        scratch[2, pl.ds(base + 2 * cp, n, stride=8), :] = c0
        scratch[2, pl.ds(base + 2 * cp + 1, n, stride=8), :] = c1

    def send_sums(u):
        osend[u] = scratch[2].reshape(16, 16, 128).astype(BF16)
        exchange1(osend.at[u], orecv.at[u], os.at[u], orr.at[u])

    project(0)
    pl.semaphore_wait(barrier, 30)
    stage1(0)
    wt[0, 4] = transposed_weight(wpb[0], 512)
    gate_of(0)
    wt[0, 5] = transposed_weight(wob[0], 0)
    stage1_wait(0, False)

    spread(0, 0)
    for cp in range(4):
        even, odd = pairs(0, 0, cp)
        la0[cp] = jnp.concatenate([even, odd], axis=0).astype(BF16)
    across = pltpu.make_async_remote_copy(
        la0, lb0.at[q], l2s.at[0], l2r.at[0], device_id=(row, over), device_id_type=MESH
    )
    across.start()
    to_mate = send_mate(la0, lb0.at[q], cs.at[0], cr.at[0])
    to_mate.start()
    lb0[q] = la0[...]
    spread(0, 1)
    for cp in range(4):
        even, odd = pairs(0, 1, cp)
        for j in range(4):
            ra0[j, cp] = jnp.concatenate(
                [even[8 * j : 8 * j + 8], odd[8 * j : 8 * j + 8]], axis=0
            ).astype(BF16)
    send_all16(ra0, rb0, r2s.at[0], r2r.at[0])
    across.wait_recv()
    passed = send_mate(lb0.at[over], lb0.at[over], cs.at[1], cr.at[1])
    passed.start()
    to_mate.wait_recv()
    wait_bytes(rb0, 15, r2s.at[0], r2r.at[0], False)
    passed.wait_recv()

    low64 = iota((64, 128), 1) < 64
    zero = jnp.zeros((64, 128), BF16)
    for cp in range(4):
        a = jnp.concatenate([lb0[k, cp] for k in range(4)], axis=1)
        cols = []
        for k in range(4):
            b = jnp.concatenate([rb0[4 * j + k, cp] for j in range(4)], axis=0)
            cols.append(
                jnp.concatenate([jnp.where(low64, b, zero), jnp.where(low64, zero, b)], axis=0)
            )
        o = dot(a, jnp.concatenate(cols, axis=1), NT)
        emit_sums(cp, o[:32], o[32:])
    send_sums(0)
    for blk in range(5):
        wt[1, blk] = transposed_weight(wpb[1], blk * 128)
    wt[1, 5] = transposed_weight(wob[1], 0)
    wait_bytes(orecv.at[0], 15, os.at[0], orr.at[0], False)
    p_t[...] = finish(0).astype(F32)

    project(1)
    stage1_left()
    direct_right()
    gate_of(1)
    wait_bytes(osend.at[0], 15, s1s.at[1], s1r.at[1], False)
    spread(1, 0)
    pick = onehot(iota((64, 128), 0) == iota((64, 128), 1) % 64)
    for cp in range(4):
        even, odd = pairs(1, 0, cp)
        m = jnp.concatenate([even, odd], axis=0).astype(BF16)
        m2 = jnp.concatenate([jnp.where(low64, m, zero), jnp.where(low64, zero, m)], axis=0)
        t = dot(pick, m2, NT).astype(BF16)
        for k in range(4):
            la1[k, cp] = t[16 * k : 16 * k + 16]
    send_left1()
    for d in range(3):
        right_from(d)
    passed1 = []
    for c in range(2):
        got = lb1.at[core, c]
        pltpu.make_async_remote_copy(
            got, got, l1s, l1r.at[c], device_id=(row, mate), device_id_type=MESH
        ).wait_recv()
        passed1.append(send_mate(got, got, cs.at[2 + c], cr.at[2 + c]))
        passed1[c].start()
        if c == 0:
            right_from(3)
        passed1[c].wait_recv()
        for cp in range(4):
            a = jnp.concatenate(
                [jnp.concatenate([lb1[k, c, j, cp] for k in range(2)], axis=0) for j in range(4)],
                axis=1,
            )
            rows = []
            for j in range(4):
                b = rb1[j, cp]
                rows += [jnp.where(low64, b, zero), jnp.where(low64, zero, b)]
            o = dot(a, jnp.concatenate(rows, axis=0), NN).reshape(2, 2, 8, 128)
            emit_sums(cp, o[:, 0].reshape(16, 128), o[:, 1].reshape(16, 128), 128 * c)
        send_sums_half(c)
    perm[...] = onehot(n0 == (n1 // 64) * 64 + column_of(n1 % 64))
    wait_bytes(orecv.at[1], 15, os.at[1], orr.at[1], False)
    final = finish(1)
    out[...] = dot(perm[...], final, NT).astype(BF16).reshape(4, 64, 128)

    stage1_wait(0, True)
    across.wait_send()
    to_mate.wait_send()
    passed.wait_send()
    wait_bytes(rb0, 15, r2s.at[0], r2r.at[0], True)
    wait_bytes(orecv.at[0], 15, os.at[0], orr.at[0], True)
    wait_bytes(osend.at[0], 15, s1s.at[1], s1r.at[1], True)
    wait_bytes(rb0, 7, l1s, l1r.at[0], True)
    for c in passed1:
        c.wait_send()
    for n in (16, 16, 16, 15):
        wait_bytes(osend.at[0], n, rds, rdr.at[0], True)
    wait_bytes(orecv.at[1], 15, os.at[1], orr.at[1], True)


def body(pair, token_mask, w_proj, w_out):
    any_spec = pl.BlockSpec(memory_space=pl.ANY)
    vm = pltpu.VMEM
    dma = pltpu.SemaphoreType.DMA
    return pl.pallas_call(
        kernel,
        out_shape=pltpu.VMEM((4, 64, 128), BF16),
        in_specs=[any_spec] * 4,
        out_specs=pl.BlockSpec(memory_space=pltpu.VMEM),
        scratch_shapes=[
            vm((4, 64, 128), BF16),
            vm((1, 256), jnp.int32),
            vm((2, 128, 640), BF16),
            vm((2, 128, 128), BF16),
            vm((2, 6, 128, 128), BF16),
            vm((128, 256), F32),
            vm((128, 256), F32),
            vm((256, 256), BF16),
            vm((2, 16, 2, 16, 128), BF16),
            vm((2, 16, 2, 16, 128), BF16),
            vm((3, 256, 128), F32),
            vm((4, 64, 128), BF16),
            vm((4, 4, 16, 128), BF16),
            vm((4, 4, 64, 128), BF16),
            vm((16, 4, 16, 128), BF16),
            vm((4, 4, 16, 128), BF16),
            vm((4, 16, 16, 128), BF16),
            vm((2, 2, 4, 4, 16, 128), BF16),
            vm((4, 4, 64, 128), BF16),
            vm((2, 16, 16, 128), BF16),
            vm((2, 16, 16, 128), BF16),
            dma((4,)),
            dma((2,)),
            dma((2,)),
            dma,
            dma((4,)),
            dma((1,)),
            dma((1,)),
            dma,
            dma((2,)),
            dma((4,)),
            dma((4,)),
        ]
        + [dma((2,))] * 4,
        compiler_params=pltpu.CompilerParams(
            collective_id=0, has_side_effects=True, vmem_limit_bytes=60 * 2**20
        ),
        name="triangles",
    )(pair, token_mask.reshape(1, 256), w_proj, w_out)


def solution(mesh):
    return jax.shard_map(
        body,
        mesh=mesh,
        in_specs=(P("row", "ka", None), P(), P(), P()),
        out_specs=P("row", "ka", None),
        check_vma=False,
    )
```

```python
import functools

import jax
import jax.numpy as jnp
from jax import lax
from jax.experimental import pallas as pl
from jax.experimental.pallas import tpu as pltpu
from jax.sharding import PartitionSpec as P

EPS = 1e-05
PE, PH, PL = 1, 4, 2
MESH = pl.DeviceIdType.MESH
FAR1 = tuple((dz, e) for dz in (4, 3, 5, 2, 6, 1, 7, 0) for e in (1, 0))[:-1]
FAR2 = (12, 13, 14, 15, 6, 7, 8, 9, 4, 5, 10, 11, 2, 3, 1)
F32 = jnp.float32
BF16 = jnp.bfloat16
NT = (((1,), (1,)), ((), ()))
NN = (((1,), (0,)), ((), ()))


def dot(a, b, dims):
    return lax.dot_general(a, b, dims, preferred_element_type=F32)


def iota(shape, axis):
    return lax.broadcasted_iota(jnp.int32, shape, axis)


def onehot(cond):
    return jnp.where(cond, 1.0, 0.0).astype(BF16)


def column_of(p):
    v = PH * (p // 32) + PL * ((p // 16) % 2) + PE * ((p // 2) % 2)
    return 32 * ((p // 4) % 2) + 4 * v + 2 * (p % 2) + (p // 8) % 2


def eye(n):
    return onehot(iota((n, n), 0) == iota((n, n), 1))


def norm_t(v):
    mean = jnp.mean(v, axis=0, keepdims=True)
    centered = v - mean
    var = jnp.mean(centered * centered, axis=0, keepdims=True)
    return centered * lax.rsqrt(var + EPS)


def transposed_weight(w, lo):
    return dot(eye(128), w[:, lo : lo + 128], NT).astype(BF16)


def tiles_of(t):
    lo = t[:, :128].reshape(16, 8, 128)
    hi = t[:, 128:].reshape(16, 8, 128)
    return jnp.concatenate([lo, hi], axis=1).astype(BF16)


def kernel(
    pair, mask, wp, wo, out,
    xb, mb, wpb, wob, wt, p_t, gate, perm,
    send1, recv1, scratch, la0, ra0, lb0, rb0, la1, rdir, lb1, rb1, osend, orecv,
    lsem, s1s, s1r, rds, rdr, l2s, l2r, l1s, l1r, cs, cr, r2s, r2r, os, orr,
):
    row = lax.axis_index("row")
    q = lax.axis_index("ka")
    z = row // 8
    lo = (row // PE) % 2
    g = z * 2 + lo
    x = ((row // PH) % 2) * 2 + (row // PL) % 2
    s = x * 4 + q
    core = q % 2
    mate = q + 1 - 2 * core
    over = (q + 2) % 4
    side = q // 2

    def row_of(group, v):
        return (group // 2) * 8 + (v // 2) * PH + (v % 2) * PL + (group % 2) * PE

    classes = [((x // 2 + f // 2) % 2) * 2 + (x + f) % 2 for f in range(4)]
    group1 = [((z + dz) % 8) * 2 + (lo + e) % 2 for dz, e in FAR1]
    group2 = []
    for m in FAR2:
        v = ((x // 2 + m // 8) % 2) * 2 + (x + m // 4) % 2
        group2.append((v, ((q // 2 + m // 2) % 2) * 2 + (q + m) % 2))

    barrier = pltpu.get_barrier_semaphore()
    for t in group1:
        pl.semaphore_signal(barrier, inc=1, device_id=(row_of(t, x), q), device_id_type=MESH)
    for v, t in group2:
        pl.semaphore_signal(barrier, inc=1, device_id=(row_of(g, v), t), device_id_type=MESH)
    loads = [
        pltpu.make_async_copy(a, b, lsem.at[i])
        for i, (a, b) in enumerate(((pair, xb), (mask, mb), (wp, wpb), (wo, wob)))
    ]
    for c in loads:
        c.start()
    for c in loads:
        c.wait()

    for blk in range(4):
        wt[0, blk] = transposed_weight(wpb[0], blk * 128)

    n0 = iota((256, 256), 0)
    n1 = iota((256, 256), 1)
    perm_t = onehot(n1 == (n0 // 64) * 64 + column_of(n0 % 64))
    moved = dot(perm_t, xb[...].reshape(256, 128), NN).astype(BF16)
    p_t[...] = dot(eye(128), moved, NT)
    tokens = jnp.broadcast_to(mb[...].astype(F32), (16, 256)).astype(BF16)
    m_row = dot(tokens, onehot(n0 == 4 * row + n1 // 64), NN)[0:1]
    m_col = dot(tokens, onehot(n0 == 64 * q + column_of(n1 % 64)), NN)[0:1]
    m_pair = m_row * m_col

    def project(u):
        normed = norm_t(p_t[...]).astype(BF16)
        ga = dot(wt[u, 0], normed, NN)
        va = dot(wt[u, 1], normed, NN)
        send1[u, :, 0] = tiles_of(jax.nn.sigmoid(ga) * va * m_pair)
        gb = dot(wt[u, 2], normed, NN)
        vb = dot(wt[u, 3], normed, NN)
        send1[u, :, 1] = tiles_of(jax.nn.sigmoid(gb) * vb * m_pair)

    def gate_of(u):
        normed = norm_t(p_t[...]).astype(BF16)
        gate[...] = jax.nn.sigmoid(dot(wt[u, 4], normed, NN))

    def exchange1(src, dst, ssem, rsem):
        for t in group1:
            pltpu.make_async_remote_copy(
                src.at[t], dst.at[g], ssem, rsem, device_id=(row_of(t, x), q), device_id_type=MESH
            ).start()
        dst[g] = src[g]

    def stage1(i):
        exchange1(send1.at[i], recv1.at[i], s1s.at[i], s1r.at[i])

    def stage1_left():
        for t in group1:
            pltpu.make_async_remote_copy(
                send1.at[1, t, 0], recv1.at[1, g, 0], s1s.at[1], s1r.at[1],
                device_id=(row_of(t, x), q), device_id_type=MESH,
            ).start()
        recv1[1, g, 0] = send1[1, g, 0]

    def direct_right():
        for d in (3, 2, 1, 0):
            v = classes[d]

            def step(i, carry):
                t = (g + 8 + ((i + 1) // 2) * (1 - 2 * (i % 2))) % 16
                pltpu.make_async_remote_copy(
                    send1.at[1, t, 1], rdir.at[x, g], rds, rdr.at[x],
                    device_id=(row_of(t, v), q), device_id_type=MESH,
                ).start()
                return carry

            lax.fori_loop(0, 15 if d == 0 else 16, step, 0)
        rdir[x, g] = send1[1, g, 1]

    def right_from(d):
        v = classes[d]
        n = 15 if d == 0 else 16
        part = osend.at[0, pl.ds(0, n)]
        pltpu.make_async_remote_copy(
            part, part, rds, rdr.at[v], device_id=(row, mate), device_id_type=MESH
        ).wait_recv()
        scratch[1] = rdir[v].astype(F32).reshape(256, 128)
        for cp in range(4):
            even, odd = pairs(1, 1, cp)
            rb1[v, cp] = jnp.concatenate([even, odd], axis=0).astype(BF16)

    def stage1_wait(i, send):
        wait_bytes(recv1.at[i], 15, s1s.at[i], s1r.at[i], send)

    def wait_bytes(buf, count, ssem, rsem, send):
        part = buf.at[pl.ds(0, count)]
        c = pltpu.make_async_remote_copy(
            part, part, ssem, rsem, device_id=(row, mate), device_id_type=MESH
        )
        if send:
            c.wait_send()
        else:
            c.wait_recv()

    low = iota((32, 128), 1) < 64

    def pairs(u, side, cp):
        f = scratch.at[side]
        xa = f[pl.ds(2 * cp, 32, stride=8), :]
        xb_ = f[pl.ds(2 * cp + 1, 32, stride=8), :]
        even = jnp.where(low, xa, pltpu.roll(xb_, 64, 1))
        odd = jnp.where(low, pltpu.roll(xa, 64, 1), xb_)
        return even, odd

    def spread(u, side):
        scratch[side] = recv1[u, :, side].astype(F32).reshape(256, 128)

    def send_mate(src, dst, ssem, rsem):
        return pltpu.make_async_remote_copy(
            src, dst, ssem, rsem, device_id=(row, mate), device_id_type=MESH
        )

    def send_all16(src, dst, ssem, rsem):
        for tx, tq in group2:
            pltpu.make_async_remote_copy(
                src.at[tq], dst.at[s], ssem, rsem, device_id=(row_of(g, tx), tq), device_id_type=MESH
            ).start()
        dst[s] = src[q]

    def send_left1():
        for v in range(4):
            for there in range(4):
                copy = pltpu.make_async_remote_copy(
                    la1.at[v], lb1.at[core, side, x], l1s, l1r.at[side],
                    device_id=(row_of(g, v), there), device_id_type=MESH,
                )
                pl.when((x != v) | (q != there))(copy.start)
        pltpu.make_async_copy(la1.at[x], lb1.at[core, side, x], l1r.at[side]).start()

    def send_sums_half(c):
        part = sums_rows(c)
        osend[1, 8 * c : 8 * c + 8] = part.reshape(8, 16, 128).astype(BF16)

        def out(t):
            return pltpu.make_async_remote_copy(
                osend.at[1, t], orecv.at[1, g], os.at[1], orr.at[1],
                device_id=(row_of(t, x), q), device_id_type=MESH,
            )

        for i in (4, 5, 3, 2, 6, 7, 1):
            out(8 * c + (g + i) % 8).start()

        @pl.when(g // 8 != c)
        def _():
            out(8 * c + g % 8).start()

        @pl.when(g // 8 == c)
        def _():
            orecv[1, g] = osend[1, g]

    def sums_rows(c):
        return scratch[2, 128 * c : 128 * c + 128]

    def finish(u):
        hb = orecv[u].astype(F32)
        summed = jnp.concatenate(
            [hb[:, :8].reshape(128, 128), hb[:, 8:].reshape(128, 128)], axis=1
        )
        xn = norm_t(summed).astype(BF16)
        upd = dot(wt[u, 5], xn, NN)
        return (p_t[...] + gate[...] * upd).astype(BF16)

    def emit_sums(cp, oa0, oa1, base=0):
        n = oa0.shape[0]
        low = iota((n, 128), 1) < 64
        c0 = jnp.where(low, oa0, pltpu.roll(oa1, 64, 1))
        c1 = jnp.where(low, pltpu.roll(oa0, 64, 1), oa1)
        scratch[2, pl.ds(base + 2 * cp, n, stride=8), :] = c0
        scratch[2, pl.ds(base + 2 * cp + 1, n, stride=8), :] = c1

    def send_sums(u):
        osend[u] = scratch[2].reshape(16, 16, 128).astype(BF16)
        exchange1(osend.at[u], orecv.at[u], os.at[u], orr.at[u])

    project(0)
    pl.semaphore_wait(barrier, 30)
    stage1(0)
    wt[0, 4] = transposed_weight(wpb[0], 512)
    gate_of(0)
    wt[0, 5] = transposed_weight(wob[0], 0)
    stage1_wait(0, False)

    spread(0, 0)
    for cp in range(4):
        even, odd = pairs(0, 0, cp)
        la0[cp] = jnp.concatenate([even, odd], axis=0).astype(BF16)
    across = pltpu.make_async_remote_copy(
        la0, lb0.at[q], l2s.at[0], l2r.at[0], device_id=(row, over), device_id_type=MESH
    )
    across.start()
    to_mate = send_mate(la0, lb0.at[q], cs.at[0], cr.at[0])
    to_mate.start()
    lb0[q] = la0[...]
    spread(0, 1)
    for cp in range(4):
        even, odd = pairs(0, 1, cp)
        for j in range(4):
            ra0[j, cp] = jnp.concatenate(
                [even[8 * j : 8 * j + 8], odd[8 * j : 8 * j + 8]], axis=0
            ).astype(BF16)
    send_all16(ra0, rb0, r2s.at[0], r2r.at[0])
    across.wait_recv()
    passed = send_mate(lb0.at[over], lb0.at[over], cs.at[1], cr.at[1])
    passed.start()
    to_mate.wait_recv()
    wait_bytes(rb0, 15, r2s.at[0], r2r.at[0], False)
    passed.wait_recv()

    low64 = iota((64, 128), 1) < 64
    zero = jnp.zeros((64, 128), BF16)
    for cp in range(4):
        a = jnp.concatenate([lb0[k, cp] for k in range(4)], axis=1)
        cols = []
        for k in range(4):
            b = jnp.concatenate([rb0[4 * j + k, cp] for j in range(4)], axis=0)
            cols.append(
                jnp.concatenate([jnp.where(low64, b, zero), jnp.where(low64, zero, b)], axis=0)
            )
        o = dot(a, jnp.concatenate(cols, axis=1), NT)
        emit_sums(cp, o[:32], o[32:])
    send_sums(0)
    for blk in range(5):
        wt[1, blk] = transposed_weight(wpb[1], blk * 128)
    wt[1, 5] = transposed_weight(wob[1], 0)
    wait_bytes(orecv.at[0], 15, os.at[0], orr.at[0], False)
    p_t[...] = finish(0).astype(F32)

    project(1)
    stage1_left()
    direct_right()
    gate_of(1)
    wait_bytes(osend.at[0], 15, s1s.at[1], s1r.at[1], False)
    spread(1, 0)
    pick = onehot(iota((64, 128), 0) == iota((64, 128), 1) % 64)
    for cp in range(4):
        even, odd = pairs(1, 0, cp)
        m = jnp.concatenate([even, odd], axis=0).astype(BF16)
        m2 = jnp.concatenate([jnp.where(low64, m, zero), jnp.where(low64, zero, m)], axis=0)
        t = dot(pick, m2, NT).astype(BF16)
        for k in range(4):
            la1[k, cp] = t[16 * k : 16 * k + 16]
    send_left1()
    for d in range(3):
        right_from(d)
    for c in range(2):
        wait_bytes(rb0, 8, l1s, l1r.at[c], False)
        if c == 0:
            right_from(3)
        for cp in range(4):
            a = jnp.concatenate(
                [jnp.concatenate([lb1[k, c, j, cp] for k in range(2)], axis=0) for j in range(4)],
                axis=1,
            )
            rows = []
            for j in range(4):
                b = rb1[j, cp]
                rows += [jnp.where(low64, b, zero), jnp.where(low64, zero, b)]
            o = dot(a, jnp.concatenate(rows, axis=0), NN).reshape(2, 2, 8, 128)
            emit_sums(cp, o[:, 0].reshape(16, 128), o[:, 1].reshape(16, 128), 128 * c)
        send_sums_half(c)
    perm[...] = onehot(n0 == (n1 // 64) * 64 + column_of(n1 % 64))
    wait_bytes(orecv.at[1], 15, os.at[1], orr.at[1], False)
    final = finish(1)
    out[...] = dot(perm[...], final, NT).astype(BF16).reshape(4, 64, 128)

    stage1_wait(0, True)
    across.wait_send()
    to_mate.wait_send()
    passed.wait_send()
    wait_bytes(rb0, 15, r2s.at[0], r2r.at[0], True)
    wait_bytes(orecv.at[0], 15, os.at[0], orr.at[0], True)
    wait_bytes(osend.at[0], 15, s1s.at[1], s1r.at[1], True)
    wait_bytes(rb0, 15, l1s, l1r.at[0], True)
    for n in (16, 16, 16, 15):
        wait_bytes(osend.at[0], n, rds, rdr.at[0], True)
    wait_bytes(orecv.at[1], 15, os.at[1], orr.at[1], True)


def body(pair, token_mask, w_proj, w_out):
    any_spec = pl.BlockSpec(memory_space=pl.ANY)
    vm = pltpu.VMEM
    dma = pltpu.SemaphoreType.DMA
    return pl.pallas_call(
        kernel,
        out_shape=pltpu.VMEM((4, 64, 128), BF16),
        in_specs=[any_spec] * 4,
        out_specs=pl.BlockSpec(memory_space=pltpu.VMEM),
        scratch_shapes=[
            vm((4, 64, 128), BF16),
            vm((1, 256), jnp.int32),
            vm((2, 128, 640), BF16),
            vm((2, 128, 128), BF16),
            vm((2, 6, 128, 128), BF16),
            vm((128, 256), F32),
            vm((128, 256), F32),
            vm((256, 256), BF16),
            vm((2, 16, 2, 16, 128), BF16),
            vm((2, 16, 2, 16, 128), BF16),
            vm((3, 256, 128), F32),
            vm((4, 64, 128), BF16),
            vm((4, 4, 16, 128), BF16),
            vm((4, 4, 64, 128), BF16),
            vm((16, 4, 16, 128), BF16),
            vm((4, 4, 16, 128), BF16),
            vm((4, 16, 16, 128), BF16),
            vm((2, 2, 4, 4, 16, 128), BF16),
            vm((4, 4, 64, 128), BF16),
            vm((2, 16, 16, 128), BF16),
            vm((2, 16, 16, 128), BF16),
            dma((4,)),
            dma((2,)),
            dma((2,)),
            dma,
            dma((4,)),
            dma((1,)),
            dma((1,)),
            dma,
            dma((2,)),
            dma((4,)),
            dma((4,)),
        ]
        + [dma((2,))] * 4,
        compiler_params=pltpu.CompilerParams(
            collective_id=0, has_side_effects=True, vmem_limit_bytes=60 * 2**20
        ),
        name="triangles",
    )(pair, token_mask.reshape(1, 256), w_proj, w_out)


def solution(mesh):
    return jax.shard_map(
        body,
        mesh=mesh,
        in_specs=(P("row", "ka", None), P(), P(), P()),
        out_specs=P("row", "ka", None),
        check_vma=False,
    )
```

```python
import functools

import jax
import jax.numpy as jnp
from jax import lax
from jax.experimental import pallas as pl
from jax.experimental.pallas import tpu as pltpu
from jax.sharding import PartitionSpec as P

EPS = 1e-05
PE, PH, PL = 1, 4, 2
MESH = pl.DeviceIdType.MESH
FAR1 = tuple((dz, e) for dz in (4, 3, 5, 2, 6, 1, 7, 0) for e in (1, 0))[:-1]
FAR2 = (12, 13, 14, 15, 6, 7, 8, 9, 4, 5, 10, 11, 2, 3, 1)
F32 = jnp.float32
BF16 = jnp.bfloat16
NT = (((1,), (1,)), ((), ()))
NN = (((1,), (0,)), ((), ()))


def dot(a, b, dims):
    return lax.dot_general(a, b, dims, preferred_element_type=F32)


def iota(shape, axis):
    return lax.broadcasted_iota(jnp.int32, shape, axis)


def onehot(cond):
    return jnp.where(cond, 1.0, 0.0).astype(BF16)


def column_of(p):
    v = PH * (p // 32) + PL * ((p // 16) % 2) + PE * ((p // 2) % 2)
    return 32 * ((p // 4) % 2) + 4 * v + 2 * (p % 2) + (p // 8) % 2


def eye(n):
    return onehot(iota((n, n), 0) == iota((n, n), 1))


def norm_t(v):
    mean = jnp.mean(v, axis=0, keepdims=True)
    centered = v - mean
    var = jnp.mean(centered * centered, axis=0, keepdims=True)
    return centered * lax.rsqrt(var + EPS)


def transposed_weight(w, lo):
    return dot(eye(128), w[:, lo : lo + 128], NT).astype(BF16)


def tiles_of(t):
    lo = t[:, :128].reshape(16, 8, 128)
    hi = t[:, 128:].reshape(16, 8, 128)
    return jnp.concatenate([lo, hi], axis=1).astype(BF16)


def kernel(
    pair, mask, wp, wo, out,
    xb, mb, wpb, wob, wt, p_t, gate, perm,
    send1, recv1, scratch, ldir, ra0, lb0, rb0, la1, rdir, lb1, rb1, osend, orecv,
    lsem, s1s, s1r, ready, lds, ldr, rds, rdr, l1s, l1r, r2s, r2r, os, orr,
):
    row = lax.axis_index("row")
    q = lax.axis_index("ka")
    z = row // 8
    lo = (row // PE) % 2
    g = z * 2 + lo
    x = ((row // PH) % 2) * 2 + (row // PL) % 2
    s = x * 4 + q
    core = q % 2
    mate = q + 1 - 2 * core
    over = (q + 2) % 4
    side = q // 2

    def row_of(group, v):
        return (group // 2) * 8 + (v // 2) * PH + (v % 2) * PL + (group % 2) * PE

    classes = [((x // 2 + f // 2) % 2) * 2 + (x + f) % 2 for f in range(4)]
    group1 = [((z + dz) % 8) * 2 + (lo + e) % 2 for dz, e in FAR1]
    group2 = []
    for m in FAR2:
        v = ((x // 2 + m // 8) % 2) * 2 + (x + m // 4) % 2
        group2.append((v, ((q // 2 + m // 2) % 2) * 2 + (q + m) % 2))

    barrier = pltpu.get_barrier_semaphore()
    for t in group1:
        pl.semaphore_signal(barrier, inc=1, device_id=(row_of(t, x), q), device_id_type=MESH)
    for v, t in group2:
        pl.semaphore_signal(barrier, inc=1, device_id=(row_of(g, v), t), device_id_type=MESH)
    loads = [
        pltpu.make_async_copy(a, b, lsem.at[i])
        for i, (a, b) in enumerate(((pair, xb), (mask, mb), (wp, wpb), (wo, wob)))
    ]
    for c in loads:
        c.start()
    for c in loads:
        c.wait()

    for blk in range(4):
        wt[0, blk] = transposed_weight(wpb[0], blk * 128)

    n0 = iota((256, 256), 0)
    n1 = iota((256, 256), 1)
    perm_t = onehot(n1 == (n0 // 64) * 64 + column_of(n0 % 64))
    moved = dot(perm_t, xb[...].reshape(256, 128), NN).astype(BF16)
    p_t[...] = dot(eye(128), moved, NT)
    tokens = jnp.broadcast_to(mb[...].astype(F32), (16, 256)).astype(BF16)
    m_row = dot(tokens, onehot(n0 == 4 * row + n1 // 64), NN)[0:1]
    m_col = dot(tokens, onehot(n0 == 64 * q + column_of(n1 % 64)), NN)[0:1]
    m_pair = m_row * m_col

    def project(u):
        normed = norm_t(p_t[...]).astype(BF16)
        ga = dot(wt[u, 0], normed, NN)
        va = dot(wt[u, 1], normed, NN)
        send1[u, :, 0] = tiles_of(jax.nn.sigmoid(ga) * va * m_pair)
        gb = dot(wt[u, 2], normed, NN)
        vb = dot(wt[u, 3], normed, NN)
        send1[u, :, 1] = tiles_of(jax.nn.sigmoid(gb) * vb * m_pair)

    def gate_of(u):
        normed = norm_t(p_t[...]).astype(BF16)
        gate[...] = jax.nn.sigmoid(dot(wt[u, 4], normed, NN))

    def exchange1(src, dst, ssem, rsem):
        for t in group1:
            pltpu.make_async_remote_copy(
                src.at[t], dst.at[g], ssem, rsem, device_id=(row_of(t, x), q), device_id_type=MESH
            ).start()
        dst[g] = src[g]

    def stage1_left():
        for t in group1:
            pltpu.make_async_remote_copy(
                send1.at[1, t, 0], recv1.at[1, g, 0], s1s.at[1], s1r.at[1],
                device_id=(row_of(t, x), q), device_id_type=MESH,
            ).start()
        recv1[1, g, 0] = send1[1, g, 0]

    def wait_tiles(n, ssem, rsem, send):
        wait_bytes(osend.at[0], n, ssem, rsem, send)

    def stage1_right():
        for t in group1:
            pltpu.make_async_remote_copy(
                send1.at[0, t, 1], recv1.at[0, g, 1], s1s.at[0], s1r.at[0],
                device_id=(row_of(t, x), q), device_id_type=MESH,
            ).start()
        recv1[0, g, 1] = send1[0, g, 1]

    def direct_left(there, n):
        def step(i, carry):
            t = (g + 8 + ((i + 1) // 2) * (1 - 2 * (i % 2))) % 16
            pltpu.make_async_remote_copy(
                send1.at[0, t, 0], ldir.at[q, g], lds, ldr.at[q],
                device_id=(row_of(t, x), there), device_id_type=MESH,
            ).start()
            return carry

        lax.fori_loop(0, n, step, 0)

    def left_from(b, n):
        wait_tiles(n, lds, ldr.at[b], False)
        scratch[0] = ldir[b].astype(F32).reshape(256, 128)
        for cp in range(4):
            even, odd = pairs(0, 0, cp)
            lb0[b, cp] = jnp.concatenate([even, odd], axis=0).astype(BF16)

    def direct_right():
        for d in (3, 2, 1, 0):
            v = classes[d]

            def step(i, carry):
                t = (g + 8 + ((i + 1) // 2) * (1 - 2 * (i % 2))) % 16
                pltpu.make_async_remote_copy(
                    send1.at[1, t, 1], rdir.at[x, g], rds, rdr.at[x],
                    device_id=(row_of(t, v), q), device_id_type=MESH,
                ).start()
                return carry

            lax.fori_loop(0, 15 if d == 0 else 16, step, 0)
        rdir[x, g] = send1[1, g, 1]

    def right_from(d):
        v = classes[d]
        n = 15 if d == 0 else 16
        part = osend.at[0, pl.ds(0, n)]
        pltpu.make_async_remote_copy(
            part, part, rds, rdr.at[v], device_id=(row, mate), device_id_type=MESH
        ).wait_recv()
        scratch[1] = rdir[v].astype(F32).reshape(256, 128)
        for cp in range(4):
            even, odd = pairs(1, 1, cp)
            rb1[v, cp] = jnp.concatenate([even, odd], axis=0).astype(BF16)

    def wait_bytes(buf, count, ssem, rsem, send):
        part = buf.at[pl.ds(0, count)]
        c = pltpu.make_async_remote_copy(
            part, part, ssem, rsem, device_id=(row, mate), device_id_type=MESH
        )
        if send:
            c.wait_send()
        else:
            c.wait_recv()

    low = iota((32, 128), 1) < 64

    def pairs(u, side, cp):
        f = scratch.at[side]
        xa = f[pl.ds(2 * cp, 32, stride=8), :]
        xb_ = f[pl.ds(2 * cp + 1, 32, stride=8), :]
        even = jnp.where(low, xa, pltpu.roll(xb_, 64, 1))
        odd = jnp.where(low, pltpu.roll(xa, 64, 1), xb_)
        return even, odd

    def spread(u, side):
        scratch[side] = recv1[u, :, side].astype(F32).reshape(256, 128)

    def send_all16(src, dst, ssem, rsem):
        for tx, tq in group2:
            pltpu.make_async_remote_copy(
                src.at[tq], dst.at[s], ssem, rsem, device_id=(row_of(g, tx), tq), device_id_type=MESH
            ).start()
        dst[s] = src[q]

    def send_left1():
        for v in range(4):
            for there in range(4):
                copy = pltpu.make_async_remote_copy(
                    la1.at[v], lb1.at[core, side, x], l1s, l1r.at[side],
                    device_id=(row_of(g, v), there), device_id_type=MESH,
                )
                pl.when((x != v) | (q != there))(copy.start)
        pltpu.make_async_copy(la1.at[x], lb1.at[core, side, x], l1r.at[side]).start()

    def send_sums_half(c):
        part = sums_rows(c)
        osend[1, 8 * c : 8 * c + 8] = part.reshape(8, 16, 128).astype(BF16)

        def out(t):
            return pltpu.make_async_remote_copy(
                osend.at[1, t], orecv.at[1, g], os.at[1], orr.at[1],
                device_id=(row_of(t, x), q), device_id_type=MESH,
            )

        for i in (4, 5, 3, 2, 6, 7, 1):
            out(8 * c + (g + i) % 8).start()

        @pl.when(g // 8 != c)
        def _():
            out(8 * c + g % 8).start()

        @pl.when(g // 8 == c)
        def _():
            orecv[1, g] = osend[1, g]

    def sums_rows(c):
        return scratch[2, 128 * c : 128 * c + 128]

    def finish(u):
        hb = orecv[u].astype(F32)
        summed = jnp.concatenate(
            [hb[:, :8].reshape(128, 128), hb[:, 8:].reshape(128, 128)], axis=1
        )
        xn = norm_t(summed).astype(BF16)
        upd = dot(wt[u, 5], xn, NN)
        return (p_t[...] + gate[...] * upd).astype(BF16)

    def emit_sums(cp, oa0, oa1, base=0):
        n = oa0.shape[0]
        low = iota((n, 128), 1) < 64
        c0 = jnp.where(low, oa0, pltpu.roll(oa1, 64, 1))
        c1 = jnp.where(low, pltpu.roll(oa0, 64, 1), oa1)
        scratch[2, pl.ds(base + 2 * cp, n, stride=8), :] = c0
        scratch[2, pl.ds(base + 2 * cp + 1, n, stride=8), :] = c1

    def send_sums(u):
        osend[u] = scratch[2].reshape(16, 16, 128).astype(BF16)
        exchange1(osend.at[u], orecv.at[u], os.at[u], orr.at[u])

    project(0)
    pl.semaphore_wait(barrier, 30)
    beside = (mate, over, (mate + 2) % 4)
    for b in beside:
        pl.semaphore_signal(ready, inc=1, device_id=(row, b), device_id_type=MESH)
    stage1_right()
    direct_left(q, 15)
    ldir[q, g] = send1[0, g, 0]
    pl.semaphore_wait(ready, 3)
    for b in (beside[2], beside[1], beside[0]):
        direct_left(b, 16)
    wt[0, 4] = transposed_weight(wpb[0], 512)
    gate_of(0)
    wt[0, 5] = transposed_weight(wob[0], 0)
    wait_tiles(15, s1s.at[0], s1r.at[0], False)

    spread(0, 1)
    for cp in range(4):
        even, odd = pairs(0, 1, cp)
        for j in range(4):
            ra0[j, cp] = jnp.concatenate(
                [even[8 * j : 8 * j + 8], odd[8 * j : 8 * j + 8]], axis=0
            ).astype(BF16)
    send_all16(ra0, rb0, r2s.at[0], r2r.at[0])
    left_from(q, 15)
    for b in beside:
        left_from(b, 16)
    wait_bytes(rb0, 15, r2s.at[0], r2r.at[0], False)

    low64 = iota((64, 128), 1) < 64
    zero = jnp.zeros((64, 128), BF16)
    for cp in range(4):
        a = jnp.concatenate([lb0[k, cp] for k in range(4)], axis=1)
        cols = []
        for k in range(4):
            b = jnp.concatenate([rb0[4 * j + k, cp] for j in range(4)], axis=0)
            cols.append(
                jnp.concatenate([jnp.where(low64, b, zero), jnp.where(low64, zero, b)], axis=0)
            )
        o = dot(a, jnp.concatenate(cols, axis=1), NT)
        emit_sums(cp, o[:32], o[32:])
    send_sums(0)
    for blk in range(5):
        wt[1, blk] = transposed_weight(wpb[1], blk * 128)
    wt[1, 5] = transposed_weight(wob[1], 0)
    wait_bytes(orecv.at[0], 15, os.at[0], orr.at[0], False)
    p_t[...] = finish(0).astype(F32)

    project(1)
    stage1_left()
    direct_right()
    gate_of(1)
    wait_bytes(osend.at[0], 15, s1s.at[1], s1r.at[1], False)
    spread(1, 0)
    pick = onehot(iota((64, 128), 0) == iota((64, 128), 1) % 64)
    for cp in range(4):
        even, odd = pairs(1, 0, cp)
        m = jnp.concatenate([even, odd], axis=0).astype(BF16)
        m2 = jnp.concatenate([jnp.where(low64, m, zero), jnp.where(low64, zero, m)], axis=0)
        t = dot(pick, m2, NT).astype(BF16)
        for k in range(4):
            la1[k, cp] = t[16 * k : 16 * k + 16]
    send_left1()
    for d in range(3):
        right_from(d)
    for c in range(2):
        wait_bytes(rb0, 8, l1s, l1r.at[c], False)
        if c == 0:
            right_from(3)
        for cp in range(4):
            a = jnp.concatenate(
                [jnp.concatenate([lb1[k, c, j, cp] for k in range(2)], axis=0) for j in range(4)],
                axis=1,
            )
            rows = []
            for j in range(4):
                b = rb1[j, cp]
                rows += [jnp.where(low64, b, zero), jnp.where(low64, zero, b)]
            o = dot(a, jnp.concatenate(rows, axis=0), NN).reshape(2, 2, 8, 128)
            emit_sums(cp, o[:, 0].reshape(16, 128), o[:, 1].reshape(16, 128), 128 * c)
        send_sums_half(c)
    perm[...] = onehot(n0 == (n1 // 64) * 64 + column_of(n1 % 64))
    wait_bytes(orecv.at[1], 15, os.at[1], orr.at[1], False)
    final = finish(1)
    out[...] = dot(perm[...], final, NT).astype(BF16).reshape(4, 64, 128)

    wait_tiles(15, s1s.at[0], s1r.at[0], True)
    for n in (16, 16, 16, 15):
        wait_tiles(n, lds, ldr.at[0], True)
    wait_bytes(rb0, 15, r2s.at[0], r2r.at[0], True)
    wait_bytes(orecv.at[0], 15, os.at[0], orr.at[0], True)
    wait_bytes(osend.at[0], 15, s1s.at[1], s1r.at[1], True)
    wait_bytes(rb0, 15, l1s, l1r.at[0], True)
    for n in (16, 16, 16, 15):
        wait_bytes(osend.at[0], n, rds, rdr.at[0], True)
    wait_bytes(orecv.at[1], 15, os.at[1], orr.at[1], True)


def body(pair, token_mask, w_proj, w_out):
    any_spec = pl.BlockSpec(memory_space=pl.ANY)
    vm = pltpu.VMEM
    dma = pltpu.SemaphoreType.DMA
    return pl.pallas_call(
        kernel,
        out_shape=pltpu.VMEM((4, 64, 128), BF16),
        in_specs=[any_spec] * 4,
        out_specs=pl.BlockSpec(memory_space=pltpu.VMEM),
        scratch_shapes=[
            vm((4, 64, 128), BF16),
            vm((1, 256), jnp.int32),
            vm((2, 128, 640), BF16),
            vm((2, 128, 128), BF16),
            vm((2, 6, 128, 128), BF16),
            vm((128, 256), F32),
            vm((128, 256), F32),
            vm((256, 256), BF16),
            vm((2, 16, 2, 16, 128), BF16),
            vm((2, 16, 2, 16, 128), BF16),
            vm((3, 256, 128), F32),
            vm((4, 16, 16, 128), BF16),
            vm((4, 4, 16, 128), BF16),
            vm((4, 4, 64, 128), BF16),
            vm((16, 4, 16, 128), BF16),
            vm((4, 4, 16, 128), BF16),
            vm((4, 16, 16, 128), BF16),
            vm((2, 2, 4, 4, 16, 128), BF16),
            vm((4, 4, 64, 128), BF16),
            vm((2, 16, 16, 128), BF16),
            vm((2, 16, 16, 128), BF16),
            dma((4,)),
            dma((2,)),
            dma((2,)),
            pltpu.SemaphoreType.REGULAR,
            dma,
            dma((4,)),
            dma,
            dma((4,)),
            dma,
            dma((2,)),
        ]
        + [dma((2,))] * 4,
        compiler_params=pltpu.CompilerParams(
            collective_id=0, has_side_effects=True, vmem_limit_bytes=60 * 2**20
        ),
        name="triangles",
    )(pair, token_mask.reshape(1, 256), w_proj, w_out)


def solution(mesh):
    return jax.shard_map(
        body,
        mesh=mesh,
        in_specs=(P("row", "ka", None), P(), P(), P()),
        out_specs=P("row", "ka", None),
        check_vma=False,
    )
```

```python
import functools

import jax
import jax.numpy as jnp
from jax import lax
from jax.experimental import pallas as pl
from jax.experimental.pallas import tpu as pltpu
from jax.sharding import PartitionSpec as P

EPS = 1e-05
PE, PH, PL = 1, 4, 2
MESH = pl.DeviceIdType.MESH
FAR1 = tuple((dz, e) for dz in (4, 3, 5, 2, 6, 1, 7, 0) for e in (1, 0))[:-1]
FAR2 = (12, 13, 14, 15, 6, 7, 8, 9, 4, 5, 10, 11, 2, 3, 1)
F32 = jnp.float32
BF16 = jnp.bfloat16
NT = (((1,), (1,)), ((), ()))
NN = (((1,), (0,)), ((), ()))


def dot(a, b, dims):
    return lax.dot_general(a, b, dims, preferred_element_type=F32)


def iota(shape, axis):
    return lax.broadcasted_iota(jnp.int32, shape, axis)


def onehot(cond):
    return jnp.where(cond, 1.0, 0.0).astype(BF16)


def column_of(p):
    v = PH * (p // 32) + PL * ((p // 16) % 2) + PE * ((p // 2) % 2)
    return 32 * ((p // 4) % 2) + 4 * v + 2 * (p % 2) + (p // 8) % 2


def eye(n):
    return onehot(iota((n, n), 0) == iota((n, n), 1))


def norm_t(v):
    mean = jnp.mean(v, axis=0, keepdims=True)
    centered = v - mean
    var = jnp.mean(centered * centered, axis=0, keepdims=True)
    return centered * lax.rsqrt(var + EPS)


def transposed_weight(w, lo):
    return dot(eye(128), w[:, lo : lo + 128], NT).astype(BF16)


def tiles_of(t):
    lo = t[:, :128].reshape(16, 8, 128)
    hi = t[:, 128:].reshape(16, 8, 128)
    return jnp.concatenate([lo, hi], axis=1).astype(BF16)


def kernel(
    pair, mask, wp, wo, out,
    xb, mb, wpb, wob, wt, p_t, gate, perm,
    send1, recv1, scratch, ldir, ra0, lb0, rb0, la1, rdir, lb1, rb1, osend, orecv,
    lsem, s1s, s1r, ready, lds, ldr, rds, rdr, l1s, l1r, r2s, r2r, os, orr,
):
    row = lax.axis_index("row")
    q = lax.axis_index("ka")
    z = row // 8
    lo = (row // PE) % 2
    g = z * 2 + lo
    x = ((row // PH) % 2) * 2 + (row // PL) % 2
    s = x * 4 + q
    core = q % 2
    mate = q + 1 - 2 * core
    over = (q + 2) % 4
    side = q // 2

    def row_of(group, v):
        return (group // 2) * 8 + (v // 2) * PH + (v % 2) * PL + (group % 2) * PE

    classes = [((x // 2 + f // 2) % 2) * 2 + (x + f) % 2 for f in range(4)]
    group1 = [((z + dz) % 8) * 2 + (lo + e) % 2 for dz, e in FAR1]
    group2 = []
    for m in FAR2:
        v = ((x // 2 + m // 8) % 2) * 2 + (x + m // 4) % 2
        group2.append((v, ((q // 2 + m // 2) % 2) * 2 + (q + m) % 2))

    barrier = pltpu.get_barrier_semaphore()
    for t in group1:
        pl.semaphore_signal(barrier, inc=1, device_id=(row_of(t, x), q), device_id_type=MESH)
    for v, t in group2:
        pl.semaphore_signal(barrier, inc=1, device_id=(row_of(g, v), t), device_id_type=MESH)
    loads = [
        pltpu.make_async_copy(a, b, lsem.at[i])
        for i, (a, b) in enumerate(((pair, xb), (mask, mb), (wp, wpb), (wo, wob)))
    ]
    for c in loads:
        c.start()
    for c in loads:
        c.wait()

    for blk in range(4):
        wt[0, blk] = transposed_weight(wpb[0], blk * 128)

    n0 = iota((256, 256), 0)
    n1 = iota((256, 256), 1)
    perm_t = onehot(n1 == (n0 // 64) * 64 + column_of(n0 % 64))
    moved = dot(perm_t, xb[...].reshape(256, 128), NN).astype(BF16)
    p_t[...] = dot(eye(128), moved, NT)
    tokens = jnp.broadcast_to(mb[...].astype(F32), (16, 256)).astype(BF16)
    m_row = dot(tokens, onehot(n0 == 4 * row + n1 // 64), NN)[0:1]
    m_col = dot(tokens, onehot(n0 == 64 * q + column_of(n1 % 64)), NN)[0:1]
    m_pair = m_row * m_col

    def project(u, normed, part):
        gate_in = dot(wt[u, 2 * part], normed, NN)
        value = dot(wt[u, 2 * part + 1], normed, NN)
        send1[u, :, part] = tiles_of(jax.nn.sigmoid(gate_in) * value * m_pair)

    def gate_of(u):
        normed = norm_t(p_t[...]).astype(BF16)
        gate[...] = jax.nn.sigmoid(dot(wt[u, 4], normed, NN))

    def exchange1(src, dst, ssem, rsem):
        for t in group1:
            pltpu.make_async_remote_copy(
                src.at[t], dst.at[g], ssem, rsem, device_id=(row_of(t, x), q), device_id_type=MESH
            ).start()
        dst[g] = src[g]

    def stage1_left():
        for t in group1:
            pltpu.make_async_remote_copy(
                send1.at[1, t, 0], recv1.at[1, g, 0], s1s.at[1], s1r.at[1],
                device_id=(row_of(t, x), q), device_id_type=MESH,
            ).start()
        recv1[1, g, 0] = send1[1, g, 0]

    def wait_tiles(n, ssem, rsem, send):
        wait_bytes(osend.at[0], n, ssem, rsem, send)

    def stage1_right():
        for t in group1:
            pltpu.make_async_remote_copy(
                send1.at[0, t, 1], recv1.at[0, g, 1], s1s.at[0], s1r.at[0],
                device_id=(row_of(t, x), q), device_id_type=MESH,
            ).start()
        recv1[0, g, 1] = send1[0, g, 1]

    def direct_left(there, n):
        def step(i, carry):
            t = (g + 8 + ((i + 1) // 2) * (1 - 2 * (i % 2))) % 16
            pltpu.make_async_remote_copy(
                send1.at[0, t, 0], ldir.at[q, g], lds, ldr.at[q],
                device_id=(row_of(t, x), there), device_id_type=MESH,
            ).start()
            return carry

        lax.fori_loop(0, n, step, 0)

    def left_from(b, n):
        wait_tiles(n, lds, ldr.at[b], False)
        scratch[0] = ldir[b].astype(F32).reshape(256, 128)
        for cp in range(4):
            even, odd = pairs(0, 0, cp)
            lb0[b, cp] = jnp.concatenate([even, odd], axis=0).astype(BF16)

    def direct_right():
        for d in (3, 2, 1, 0):
            v = classes[d]

            def step(i, carry):
                t = (g + 8 + ((i + 1) // 2) * (1 - 2 * (i % 2))) % 16
                pltpu.make_async_remote_copy(
                    send1.at[1, t, 1], rdir.at[x, g], rds, rdr.at[x],
                    device_id=(row_of(t, v), q), device_id_type=MESH,
                ).start()
                return carry

            lax.fori_loop(0, 15 if d == 0 else 16, step, 0)
        rdir[x, g] = send1[1, g, 1]

    def right_from(d):
        v = classes[d]
        n = 15 if d == 0 else 16
        part = osend.at[0, pl.ds(0, n)]
        pltpu.make_async_remote_copy(
            part, part, rds, rdr.at[v], device_id=(row, mate), device_id_type=MESH
        ).wait_recv()
        scratch[1] = rdir[v].astype(F32).reshape(256, 128)
        for cp in range(4):
            even, odd = pairs(1, 1, cp)
            rb1[v, cp] = jnp.concatenate([even, odd], axis=0).astype(BF16)

    def wait_bytes(buf, count, ssem, rsem, send):
        part = buf.at[pl.ds(0, count)]
        c = pltpu.make_async_remote_copy(
            part, part, ssem, rsem, device_id=(row, mate), device_id_type=MESH
        )
        if send:
            c.wait_send()
        else:
            c.wait_recv()

    low = iota((32, 128), 1) < 64

    def pairs(u, side, cp):
        f = scratch.at[side]
        xa = f[pl.ds(2 * cp, 32, stride=8), :]
        xb_ = f[pl.ds(2 * cp + 1, 32, stride=8), :]
        even = jnp.where(low, xa, pltpu.roll(xb_, 64, 1))
        odd = jnp.where(low, pltpu.roll(xa, 64, 1), xb_)
        return even, odd

    def spread(u, side):
        scratch[side] = recv1[u, :, side].astype(F32).reshape(256, 128)

    def send_all16(src, dst, ssem, rsem):
        for tx, tq in group2:
            pltpu.make_async_remote_copy(
                src.at[tq], dst.at[s], ssem, rsem, device_id=(row_of(g, tx), tq), device_id_type=MESH
            ).start()
        dst[s] = src[q]

    def send_left1():
        for v in range(4):
            for there in range(4):
                copy = pltpu.make_async_remote_copy(
                    la1.at[v], lb1.at[core, side, x], l1s, l1r.at[side],
                    device_id=(row_of(g, v), there), device_id_type=MESH,
                )
                pl.when((x != v) | (q != there))(copy.start)
        pltpu.make_async_copy(la1.at[x], lb1.at[core, side, x], l1r.at[side]).start()

    def send_sums_half(c):
        part = sums_rows(c)
        osend[1, 8 * c : 8 * c + 8] = part.reshape(8, 16, 128).astype(BF16)

        def out(t):
            return pltpu.make_async_remote_copy(
                osend.at[1, t], orecv.at[1, g], os.at[1], orr.at[1],
                device_id=(row_of(t, x), q), device_id_type=MESH,
            )

        for i in (4, 5, 3, 2, 6, 7, 1):
            out(8 * c + (g + i) % 8).start()

        @pl.when(g // 8 != c)
        def _():
            out(8 * c + g % 8).start()

        @pl.when(g // 8 == c)
        def _():
            orecv[1, g] = osend[1, g]

    def sums_rows(c):
        return scratch[2, 128 * c : 128 * c + 128]

    def finish(u):
        hb = orecv[u].astype(F32)
        summed = jnp.concatenate(
            [hb[:, :8].reshape(128, 128), hb[:, 8:].reshape(128, 128)], axis=1
        )
        xn = norm_t(summed).astype(BF16)
        upd = dot(wt[u, 5], xn, NN)
        return (p_t[...] + gate[...] * upd).astype(BF16)

    def emit_sums(cp, oa0, oa1, base=0):
        n = oa0.shape[0]
        low = iota((n, 128), 1) < 64
        c0 = jnp.where(low, oa0, pltpu.roll(oa1, 64, 1))
        c1 = jnp.where(low, pltpu.roll(oa0, 64, 1), oa1)
        scratch[2, pl.ds(base + 2 * cp, n, stride=8), :] = c0
        scratch[2, pl.ds(base + 2 * cp + 1, n, stride=8), :] = c1

    def send_sums(u):
        osend[u] = scratch[2].reshape(16, 16, 128).astype(BF16)
        exchange1(osend.at[u], orecv.at[u], os.at[u], orr.at[u])

    normed0 = norm_t(p_t[...]).astype(BF16)
    project(0, normed0, 0)
    project(0, normed0, 1)
    pl.semaphore_wait(barrier, 30)
    beside = (mate, over, (mate + 2) % 4)
    for b in beside:
        pl.semaphore_signal(ready, inc=1, device_id=(row, b), device_id_type=MESH)
    stage1_right()
    direct_left(q, 15)
    ldir[q, g] = send1[0, g, 0]
    pl.semaphore_wait(ready, 3)
    for b in (beside[2], beside[1], beside[0]):
        direct_left(b, 16)
    wt[0, 4] = transposed_weight(wpb[0], 512)
    gate_of(0)
    wt[0, 5] = transposed_weight(wob[0], 0)
    wait_tiles(15, s1s.at[0], s1r.at[0], False)

    spread(0, 1)
    for cp in range(4):
        even, odd = pairs(0, 1, cp)
        for j in range(4):
            ra0[j, cp] = jnp.concatenate(
                [even[8 * j : 8 * j + 8], odd[8 * j : 8 * j + 8]], axis=0
            ).astype(BF16)
    send_all16(ra0, rb0, r2s.at[0], r2r.at[0])
    left_from(q, 15)
    for b in beside:
        left_from(b, 16)
    wait_bytes(rb0, 15, r2s.at[0], r2r.at[0], False)

    low64 = iota((64, 128), 1) < 64
    zero = jnp.zeros((64, 128), BF16)
    for cp in range(4):
        a = jnp.concatenate([lb0[k, cp] for k in range(4)], axis=1)
        cols = []
        for k in range(4):
            b = jnp.concatenate([rb0[4 * j + k, cp] for j in range(4)], axis=0)
            cols.append(
                jnp.concatenate([jnp.where(low64, b, zero), jnp.where(low64, zero, b)], axis=0)
            )
        o = dot(a, jnp.concatenate(cols, axis=1), NT)
        emit_sums(cp, o[:32], o[32:])
    send_sums(0)
    for blk in range(5):
        wt[1, blk] = transposed_weight(wpb[1], blk * 128)
    wt[1, 5] = transposed_weight(wob[1], 0)
    wait_bytes(orecv.at[0], 15, os.at[0], orr.at[0], False)
    p_t[...] = finish(0).astype(F32)

    normed1 = norm_t(p_t[...]).astype(BF16)
    project(1, normed1, 0)
    stage1_left()
    project(1, normed1, 1)
    direct_right()
    gate_of(1)
    wait_bytes(osend.at[0], 15, s1s.at[1], s1r.at[1], False)
    spread(1, 0)
    pick = onehot(iota((64, 128), 0) == iota((64, 128), 1) % 64)
    for cp in range(4):
        even, odd = pairs(1, 0, cp)
        m = jnp.concatenate([even, odd], axis=0).astype(BF16)
        m2 = jnp.concatenate([jnp.where(low64, m, zero), jnp.where(low64, zero, m)], axis=0)
        t = dot(pick, m2, NT).astype(BF16)
        for k in range(4):
            la1[k, cp] = t[16 * k : 16 * k + 16]
    send_left1()
    for d in range(3):
        right_from(d)
    for c in range(2):
        wait_bytes(rb0, 8, l1s, l1r.at[c], False)
        if c == 0:
            right_from(3)
        for cp in range(4):
            a = jnp.concatenate(
                [jnp.concatenate([lb1[k, c, j, cp] for k in range(2)], axis=0) for j in range(4)],
                axis=1,
            )
            rows = []
            for j in range(4):
                b = rb1[j, cp]
                rows += [jnp.where(low64, b, zero), jnp.where(low64, zero, b)]
            o = dot(a, jnp.concatenate(rows, axis=0), NN).reshape(2, 2, 8, 128)
            emit_sums(cp, o[:, 0].reshape(16, 128), o[:, 1].reshape(16, 128), 128 * c)
        send_sums_half(c)
    perm[...] = onehot(n0 == (n1 // 64) * 64 + column_of(n1 % 64))
    wait_bytes(orecv.at[1], 15, os.at[1], orr.at[1], False)
    final = finish(1)
    out[...] = dot(perm[...], final, NT).astype(BF16).reshape(4, 64, 128)

    wait_tiles(15, s1s.at[0], s1r.at[0], True)
    for n in (16, 16, 16, 15):
        wait_tiles(n, lds, ldr.at[0], True)
    wait_bytes(rb0, 15, r2s.at[0], r2r.at[0], True)
    wait_bytes(orecv.at[0], 15, os.at[0], orr.at[0], True)
    wait_bytes(osend.at[0], 15, s1s.at[1], s1r.at[1], True)
    wait_bytes(rb0, 15, l1s, l1r.at[0], True)
    for n in (16, 16, 16, 15):
        wait_bytes(osend.at[0], n, rds, rdr.at[0], True)
    wait_bytes(orecv.at[1], 15, os.at[1], orr.at[1], True)


def body(pair, token_mask, w_proj, w_out):
    any_spec = pl.BlockSpec(memory_space=pl.ANY)
    vm = pltpu.VMEM
    dma = pltpu.SemaphoreType.DMA
    return pl.pallas_call(
        kernel,
        out_shape=pltpu.VMEM((4, 64, 128), BF16),
        in_specs=[any_spec] * 4,
        out_specs=pl.BlockSpec(memory_space=pltpu.VMEM),
        scratch_shapes=[
            vm((4, 64, 128), BF16),
            vm((1, 256), jnp.int32),
            vm((2, 128, 640), BF16),
            vm((2, 128, 128), BF16),
            vm((2, 6, 128, 128), BF16),
            vm((128, 256), F32),
            vm((128, 256), F32),
            vm((256, 256), BF16),
            vm((2, 16, 2, 16, 128), BF16),
            vm((2, 16, 2, 16, 128), BF16),
            vm((3, 256, 128), F32),
            vm((4, 16, 16, 128), BF16),
            vm((4, 4, 16, 128), BF16),
            vm((4, 4, 64, 128), BF16),
            vm((16, 4, 16, 128), BF16),
            vm((4, 4, 16, 128), BF16),
            vm((4, 16, 16, 128), BF16),
            vm((2, 2, 4, 4, 16, 128), BF16),
            vm((4, 4, 64, 128), BF16),
            vm((2, 16, 16, 128), BF16),
            vm((2, 16, 16, 128), BF16),
            dma((4,)),
            dma((2,)),
            dma((2,)),
            pltpu.SemaphoreType.REGULAR,
            dma,
            dma((4,)),
            dma,
            dma((4,)),
            dma,
            dma((2,)),
        ]
        + [dma((2,))] * 4,
        compiler_params=pltpu.CompilerParams(
            collective_id=0, has_side_effects=True, vmem_limit_bytes=60 * 2**20
        ),
        name="triangles",
    )(pair, token_mask.reshape(1, 256), w_proj, w_out)


def solution(mesh):
    return jax.shard_map(
        body,
        mesh=mesh,
        in_specs=(P("row", "ka", None), P(), P(), P()),
        out_specs=P("row", "ka", None),
        check_vma=False,
    )
```

```python
import functools

import jax
import jax.numpy as jnp
from jax import lax
from jax.experimental import pallas as pl
from jax.experimental.pallas import tpu as pltpu
from jax.sharding import PartitionSpec as P

EPS = 1e-05
PE, PH, PL = 1, 4, 2
MESH = pl.DeviceIdType.MESH
FAR1 = tuple((dz, e) for dz in (4, 3, 5, 2, 6, 1, 7, 0) for e in (1, 0))[:-1]
FAR2 = (12, 13, 14, 15, 6, 7, 8, 9, 4, 5, 10, 11, 2, 3, 1)
F32 = jnp.float32
BF16 = jnp.bfloat16
NT = (((1,), (1,)), ((), ()))
NN = (((1,), (0,)), ((), ()))


def dot(a, b, dims):
    return lax.dot_general(a, b, dims, preferred_element_type=F32)


def iota(shape, axis):
    return lax.broadcasted_iota(jnp.int32, shape, axis)


def onehot(cond):
    return jnp.where(cond, 1.0, 0.0).astype(BF16)


def column_of(p):
    v = PH * (p // 32) + PL * ((p // 16) % 2) + PE * ((p // 2) % 2)
    return 32 * ((p // 4) % 2) + 4 * v + 2 * (p % 2) + (p // 8) % 2


def eye(n):
    return onehot(iota((n, n), 0) == iota((n, n), 1))


def norm_t(v):
    mean = jnp.mean(v, axis=0, keepdims=True)
    centered = v - mean
    var = jnp.mean(centered * centered, axis=0, keepdims=True)
    return centered * lax.rsqrt(var + EPS)


def transposed_weight(w, lo):
    return dot(eye(128), w[:, lo : lo + 128], NT).astype(BF16)


def tiles_of(t):
    lo = t[:, :128].reshape(16, 8, 128)
    hi = t[:, 128:].reshape(16, 8, 128)
    return jnp.concatenate([lo, hi], axis=1).astype(BF16)


def kernel(
    pair, mask, wp, wo, out,
    xb, mb, wpb, wob, wt, p_t, gate, perm,
    send1, recv1, scratch, ldir, ra0, lb0, rb0, la1, rdir, lb1, rb1, osend, orecv,
    lsem, s1s, s1r, ready, lds, ldr, rds, rdr, l1s, l1r, r2s, r2r, os, orr,
):
    row = lax.axis_index("row")
    q = lax.axis_index("ka")
    z = row // 8
    lo = (row // PE) % 2
    g = z * 2 + lo
    x = ((row // PH) % 2) * 2 + (row // PL) % 2
    s = x * 4 + q
    core = q % 2
    mate = q + 1 - 2 * core
    over = (q + 2) % 4
    side = q // 2

    def row_of(group, v):
        return (group // 2) * 8 + (v // 2) * PH + (v % 2) * PL + (group % 2) * PE

    classes = [((x // 2 + f // 2) % 2) * 2 + (x + f) % 2 for f in range(4)]
    group1 = [((z + dz) % 8) * 2 + (lo + e) % 2 for dz, e in FAR1]
    group2 = []
    for m in FAR2:
        v = ((x // 2 + m // 8) % 2) * 2 + (x + m // 4) % 2
        group2.append((v, ((q // 2 + m // 2) % 2) * 2 + (q + m) % 2))

    barrier = pltpu.get_barrier_semaphore()
    for t in group1:
        pl.semaphore_signal(barrier, inc=1, device_id=(row_of(t, x), q), device_id_type=MESH)
    for v, t in group2:
        pl.semaphore_signal(barrier, inc=1, device_id=(row_of(g, v), t), device_id_type=MESH)
    loads = [
        pltpu.make_async_copy(a, b, lsem.at[i])
        for i, (a, b) in enumerate(((pair, xb), (mask, mb), (wp, wpb), (wo, wob)))
    ]
    for c in loads:
        c.start()
    for c in loads:
        c.wait()

    for blk in range(4):
        wt[0, blk] = transposed_weight(wpb[0], blk * 128)

    n0 = iota((256, 256), 0)
    n1 = iota((256, 256), 1)
    perm_t = onehot(n1 == (n0 // 64) * 64 + column_of(n0 % 64))
    moved = dot(perm_t, xb[...].reshape(256, 128), NN).astype(BF16)
    p_t[...] = dot(eye(128), moved, NT)
    tokens = jnp.broadcast_to(mb[...].astype(F32), (16, 256)).astype(BF16)
    m_row = dot(tokens, onehot(n0 == 4 * row + n1 // 64), NN)[0:1]
    m_col = dot(tokens, onehot(n0 == 64 * q + column_of(n1 % 64)), NN)[0:1]
    m_pair = m_row * m_col

    def project(u, normed, part):
        gate_in = dot(wt[u, 2 * part], normed, NN)
        value = dot(wt[u, 2 * part + 1], normed, NN)
        send1[u, :, part] = tiles_of(jax.nn.sigmoid(gate_in) * value * m_pair)

    def gate_of(u):
        normed = norm_t(p_t[...]).astype(BF16)
        gate[...] = jax.nn.sigmoid(dot(wt[u, 4], normed, NN))

    def exchange1(src, dst, ssem, rsem):
        for t in group1:
            pltpu.make_async_remote_copy(
                src.at[t], dst.at[g], ssem, rsem, device_id=(row_of(t, x), q), device_id_type=MESH
            ).start()
        dst[g] = src[g]

    def stage1_left():
        for t in group1:
            pltpu.make_async_remote_copy(
                send1.at[1, t, 0], recv1.at[1, g, 0], s1s.at[1], s1r.at[1],
                device_id=(row_of(t, x), q), device_id_type=MESH,
            ).start()
        recv1[1, g, 0] = send1[1, g, 0]

    def wait_tiles(n, ssem, rsem, send):
        wait_bytes(osend.at[0], n, ssem, rsem, send)

    def stage1_right():
        for t in group1:
            pltpu.make_async_remote_copy(
                send1.at[0, t, 1], recv1.at[0, g, 1], s1s.at[0], s1r.at[0],
                device_id=(row_of(t, x), q), device_id_type=MESH,
            ).start()
        recv1[0, g, 1] = send1[0, g, 1]

    def direct_left(there, n):
        def step(i, carry):
            t = (g + 8 + ((i + 1) // 2) * (1 - 2 * (i % 2))) % 16
            pltpu.make_async_remote_copy(
                send1.at[0, t, 0], ldir.at[q, g], lds, ldr.at[q],
                device_id=(row_of(t, x), there), device_id_type=MESH,
            ).start()
            return carry

        lax.fori_loop(0, n, step, 0)

    def left_from(b, n):
        wait_tiles(n, lds, ldr.at[b], False)
        scratch[0] = ldir[b].astype(F32).reshape(256, 128)
        for cp in range(4):
            even, odd = pairs(0, 0, cp)
            lb0[b, cp] = jnp.concatenate([even, odd], axis=0).astype(BF16)

    def direct_right():
        for d in (3, 2, 1, 0):
            v = classes[d]

            def step(i, carry):
                t = (g + 8 + ((i + 1) // 2) * (1 - 2 * (i % 2))) % 16
                pltpu.make_async_remote_copy(
                    send1.at[1, t, 1], rdir.at[x, g], rds, rdr.at[x],
                    device_id=(row_of(t, v), q), device_id_type=MESH,
                ).start()
                return carry

            lax.fori_loop(0, 15 if d == 0 else 16, step, 0)
        rdir[x, g] = send1[1, g, 1]

    def right_from(d):
        v = classes[d]
        n = 15 if d == 0 else 16
        part = osend.at[0, pl.ds(0, n)]
        pltpu.make_async_remote_copy(
            part, part, rds, rdr.at[v], device_id=(row, mate), device_id_type=MESH
        ).wait_recv()
        scratch[1] = rdir[v].astype(F32).reshape(256, 128)
        for cp in range(4):
            even, odd = pairs(1, 1, cp)
            rb1[v, cp] = jnp.concatenate([even, odd], axis=0).astype(BF16)

    def wait_bytes(buf, count, ssem, rsem, send):
        part = buf.at[pl.ds(0, count)]
        c = pltpu.make_async_remote_copy(
            part, part, ssem, rsem, device_id=(row, mate), device_id_type=MESH
        )
        if send:
            c.wait_send()
        else:
            c.wait_recv()

    low = iota((32, 128), 1) < 64

    def pairs(u, side, cp):
        f = scratch.at[side]
        xa = f[pl.ds(2 * cp, 32, stride=8), :]
        xb_ = f[pl.ds(2 * cp + 1, 32, stride=8), :]
        even = jnp.where(low, xa, pltpu.roll(xb_, 64, 1))
        odd = jnp.where(low, pltpu.roll(xa, 64, 1), xb_)
        return even, odd

    def spread(u, side):
        scratch[side] = recv1[u, :, side].astype(F32).reshape(256, 128)

    def send_all16(src, dst, ssem, rsem):
        for tx, tq in group2:
            pltpu.make_async_remote_copy(
                src.at[tq], dst.at[s], ssem, rsem, device_id=(row_of(g, tx), tq), device_id_type=MESH
            ).start()
        dst[s] = src[q]

    def send_left1():
        for v in range(4):
            for there in range(4):
                copy = pltpu.make_async_remote_copy(
                    la1.at[v], lb1.at[core, side, x], l1s, l1r.at[side],
                    device_id=(row_of(g, v), there), device_id_type=MESH,
                )
                pl.when((x != v) | (q != there))(copy.start)
        pltpu.make_async_copy(la1.at[x], lb1.at[core, side, x], l1r.at[side]).start()

    def send_sums_half(c):
        part = sums_rows(c)
        osend[1, 8 * c : 8 * c + 8] = part.reshape(8, 16, 128).astype(BF16)

        def out(t):
            return pltpu.make_async_remote_copy(
                osend.at[1, t], orecv.at[1, g], os.at[1], orr.at[1],
                device_id=(row_of(t, x), q), device_id_type=MESH,
            )

        for i in (4, 5, 3, 2, 6, 7, 1):
            out(8 * c + (g + i) % 8).start()

        @pl.when(g // 8 != c)
        def _():
            out(8 * c + g % 8).start()

        @pl.when(g // 8 == c)
        def _():
            orecv[1, g] = osend[1, g]

    def sums_rows(c):
        return scratch[2, 128 * c : 128 * c + 128]

    def finish(u):
        hb = orecv[u].astype(F32)
        summed = jnp.concatenate(
            [hb[:, :8].reshape(128, 128), hb[:, 8:].reshape(128, 128)], axis=1
        )
        xn = norm_t(summed).astype(BF16)
        upd = dot(wt[u, 5], xn, NN)
        return (p_t[...] + gate[...] * upd).astype(BF16)

    def emit_sums(cp, oa0, oa1, base=0):
        n = oa0.shape[0]
        low = iota((n, 128), 1) < 64
        c0 = jnp.where(low, oa0, pltpu.roll(oa1, 64, 1))
        c1 = jnp.where(low, pltpu.roll(oa0, 64, 1), oa1)
        scratch[2, pl.ds(base + 2 * cp, n, stride=8), :] = c0
        scratch[2, pl.ds(base + 2 * cp + 1, n, stride=8), :] = c1

    def send_sums(u):
        osend[u] = scratch[2].reshape(16, 16, 128).astype(BF16)
        exchange1(osend.at[u], orecv.at[u], os.at[u], orr.at[u])

    normed0 = norm_t(p_t[...]).astype(BF16)
    project(0, normed0, 0)
    project(0, normed0, 1)
    pl.semaphore_wait(barrier, 30)
    beside = (mate, over, (mate + 2) % 4)
    for b in beside:
        pl.semaphore_signal(ready, inc=1, device_id=(row, b), device_id_type=MESH)
    stage1_right()
    direct_left(q, 15)
    ldir[q, g] = send1[0, g, 0]
    pl.semaphore_wait(ready, 3)
    for b in (beside[2], beside[1], beside[0]):
        direct_left(b, 16)
    wt[0, 4] = transposed_weight(wpb[0], 512)
    gate_of(0)
    wt[0, 5] = transposed_weight(wob[0], 0)
    wait_tiles(15, s1s.at[0], s1r.at[0], False)

    spread(0, 1)
    for cp in range(4):
        even, odd = pairs(0, 1, cp)
        for j in range(4):
            ra0[j, cp] = jnp.concatenate(
                [even[8 * j : 8 * j + 8], odd[8 * j : 8 * j + 8]], axis=0
            ).astype(BF16)
    send_all16(ra0, rb0, r2s.at[0], r2r.at[0])
    left_from(q, 15)
    for b in beside:
        left_from(b, 16)
    wait_bytes(rb0, 15, r2s.at[0], r2r.at[0], False)

    low64 = iota((64, 128), 1) < 64
    zero = jnp.zeros((64, 128), BF16)
    for cp in range(4):
        a = jnp.concatenate([lb0[k, cp] for k in range(4)], axis=1)
        cols = []
        for k in range(4):
            b = jnp.concatenate([rb0[4 * j + k, cp] for j in range(4)], axis=0)
            cols.append(
                jnp.concatenate([jnp.where(low64, b, zero), jnp.where(low64, zero, b)], axis=0)
            )
        o = dot(a, jnp.concatenate(cols, axis=1), NT)
        emit_sums(cp, o[:32], o[32:])
    send_sums(0)
    for blk in range(5):
        wt[1, blk] = transposed_weight(wpb[1], blk * 128)
    wt[1, 5] = transposed_weight(wob[1], 0)
    wait_bytes(orecv.at[0], 15, os.at[0], orr.at[0], False)
    p_t[...] = finish(0).astype(F32)

    normed1 = norm_t(p_t[...]).astype(BF16)
    project(1, normed1, 0)
    stage1_left()
    project(1, normed1, 1)
    direct_right()
    gate_of(1)
    wait_bytes(osend.at[0], 15, s1s.at[1], s1r.at[1], False)
    spread(1, 0)
    pick = onehot(iota((64, 128), 0) == iota((64, 128), 1) % 64)
    for cp in range(4):
        even, odd = pairs(1, 0, cp)
        m = jnp.concatenate([even, odd], axis=0).astype(BF16)
        m2 = jnp.concatenate([jnp.where(low64, m, zero), jnp.where(low64, zero, m)], axis=0)
        t = dot(pick, m2, NT).astype(BF16)
        for k in range(4):
            la1[k, cp] = t[16 * k : 16 * k + 16]
    send_left1()
    for d in range(3):
        right_from(d)
    right_from(3)
    for c in range(2):
        wait_bytes(rb0, 8, l1s, l1r.at[c], False)
        for cp in range(4):
            a = jnp.concatenate(
                [jnp.concatenate([lb1[k, c, j, cp] for k in range(2)], axis=0) for j in range(4)],
                axis=1,
            )
            rows = []
            for j in range(4):
                b = rb1[j, cp]
                rows += [jnp.where(low64, b, zero), jnp.where(low64, zero, b)]
            o = dot(a, jnp.concatenate(rows, axis=0), NN).reshape(2, 2, 8, 128)
            emit_sums(cp, o[:, 0].reshape(16, 128), o[:, 1].reshape(16, 128), 128 * c)
        send_sums_half(c)
    perm[...] = onehot(n0 == (n1 // 64) * 64 + column_of(n1 % 64))
    wait_bytes(orecv.at[1], 15, os.at[1], orr.at[1], False)
    final = finish(1)
    out[...] = dot(perm[...], final, NT).astype(BF16).reshape(4, 64, 128)

    wait_tiles(15, s1s.at[0], s1r.at[0], True)
    for n in (16, 16, 16, 15):
        wait_tiles(n, lds, ldr.at[0], True)
    wait_bytes(rb0, 15, r2s.at[0], r2r.at[0], True)
    wait_bytes(orecv.at[0], 15, os.at[0], orr.at[0], True)
    wait_bytes(osend.at[0], 15, s1s.at[1], s1r.at[1], True)
    wait_bytes(rb0, 15, l1s, l1r.at[0], True)
    for n in (16, 16, 16, 15):
        wait_bytes(osend.at[0], n, rds, rdr.at[0], True)
    wait_bytes(orecv.at[1], 15, os.at[1], orr.at[1], True)


def body(pair, token_mask, w_proj, w_out):
    any_spec = pl.BlockSpec(memory_space=pl.ANY)
    vm = pltpu.VMEM
    dma = pltpu.SemaphoreType.DMA
    return pl.pallas_call(
        kernel,
        out_shape=pltpu.VMEM((4, 64, 128), BF16),
        in_specs=[any_spec] * 4,
        out_specs=pl.BlockSpec(memory_space=pltpu.VMEM),
        scratch_shapes=[
            vm((4, 64, 128), BF16),
            vm((1, 256), jnp.int32),
            vm((2, 128, 640), BF16),
            vm((2, 128, 128), BF16),
            vm((2, 6, 128, 128), BF16),
            vm((128, 256), F32),
            vm((128, 256), F32),
            vm((256, 256), BF16),
            vm((2, 16, 2, 16, 128), BF16),
            vm((2, 16, 2, 16, 128), BF16),
            vm((3, 256, 128), F32),
            vm((4, 16, 16, 128), BF16),
            vm((4, 4, 16, 128), BF16),
            vm((4, 4, 64, 128), BF16),
            vm((16, 4, 16, 128), BF16),
            vm((4, 4, 16, 128), BF16),
            vm((4, 16, 16, 128), BF16),
            vm((2, 2, 4, 4, 16, 128), BF16),
            vm((4, 4, 64, 128), BF16),
            vm((2, 16, 16, 128), BF16),
            vm((2, 16, 16, 128), BF16),
            dma((4,)),
            dma((2,)),
            dma((2,)),
            pltpu.SemaphoreType.REGULAR,
            dma,
            dma((4,)),
            dma,
            dma((4,)),
            dma,
            dma((2,)),
        ]
        + [dma((2,))] * 4,
        compiler_params=pltpu.CompilerParams(
            collective_id=0, has_side_effects=True, vmem_limit_bytes=60 * 2**20
        ),
        name="triangles",
    )(pair, token_mask.reshape(1, 256), w_proj, w_out)


def solution(mesh):
    return jax.shard_map(
        body,
        mesh=mesh,
        in_specs=(P("row", "ka", None), P(), P(), P()),
        out_specs=P("row", "ka", None),
        check_vma=False,
    )
```
